1024 devices in a mesh: dp: 8 (over x), ctx: 32 (over y, z_hi), tp: 4 (over z_lo, core).
Axes of the slice: x: 8, y: 8, z: 8 (z_hi: 4, z_lo: 2; z = z_hi * 2 + z_lo), core: 2. Of those that a mesh axis runs over, the one named last changes fastest.
Arguments:
- tokens: bfloat16 [32768, 4096], P(('dp', 'ctx'), 'tp'), may hold values from -6 to 6
- cotangent: bfloat16 [32768, 4096], P(('dp', 'ctx'), 'tp'), may hold values from -0.375 to 0.375
- combine_weights: bfloat16 [32768, 2], P(('dp', 'ctx')), may hold values from 0.19921875 to 1
- routes: int32 [32768, 2], P(('dp', 'ctx')), may hold values from 0 to 31, all different within a row; in each aligned block of 128 rows (0 to 127, 128 to 255, ...) at most 10 rows name the same one
- w_gate: bfloat16 [32, 4096, 768], P('ctx', 'tp'), may hold values from -0.09375 to 0.09375
- w_up: bfloat16 [32, 4096, 768], P('ctx', 'tp'), may hold values from -0.09375 to 0.09375
- w_down: bfloat16 [32, 768, 4096], P('ctx', None, 'tp'), may hold values from -0.21875 to 0.21875
Outputs:
- mixed: bfloat16 [32768, 4096], P(('dp', 'ctx'), 'tp')
- combine_grads: bfloat16 [32768, 2], P(('dp', 'ctx'))
- grad_gate: float32 [32, 4096, 768], P('ctx', 'tp', 'dp')
- grad_up: float32 [32, 4096, 768], P('ctx', 'tp', 'dp')
The draws below stay inside these ranges and needn't reach their ends.
Inputs may be any that keep to these rules, and one draw needn't show every extreme that they name: `routes`: each row names 2 different experts. In each aligned block of 128 rows (the rows of one index of dp+ctx) no expert is named by more than 10 rows, a bound that some block reaches.
All inputs are finite; a program needn't handle non-finite values.
Results may differ from the reference program's by a relative error of at most 0.027.
Values may be sent and summed in bfloat16 or wider, within the bound.
No kernel may reach another device: no remote copies, remote signals or barrier semaphores. Data moves between devices by JAX's collectives and lax.ppermute only.
A program may use at most 32 MiB of HBM per device.

```python
import math
import jax
import jax.numpy as jnp
import numpy as np
from jax import lax

D = 4096
FF = 768
TOP = 2
TOK_DEV = 128
EXPERTS = 32
CAP = 10
TOKENS = 32768
N_DP = 8
N_CTX = 32
N_TP = 4


def levels(stream_key, extent, pieces, least, high):
    factor_of = 1.0
    for axis_at, shards_of in pieces:
        steps = jax.random.uniform(jax.random.fold_in(jax.random.fold_in(stream_key, 6), axis_at), (shards_of,), jnp.float32, least / len(pieces), high / len(pieces))
        factor_of = factor_of * jnp.repeat(jnp.exp(steps), extent[axis_at] // shards_of).reshape((-1,) + (1,) * (len(extent) - 1 - axis_at))
    return factor_of


def assign_block(rng, own, number, rows, number_of, top, limit, lean):
    order = jax.random.permutation(rng, number_of)
    packed, ordinary = shares(number_of, rows * top, limit, lean, True), shares(number_of, rows * top, limit, lean, False)
    places = jnp.arange(number_of)

    def named(lengths, turn):
        used = int((lengths > 0).sum())
        fixed = max(1, used // 4)
        passed = fixed + (places - fixed + turn * (used - fixed)) % max(1, number_of - fixed)
        return jnp.zeros((number_of,), jnp.int32).at[order[jnp.where(places < fixed, places, passed)]].set(jnp.asarray(lengths, jnp.int32))

    lengths = jnp.where(number % 4 == 0, named(packed, number // 4), named(ordinary, number - number // 4 - 1))
    mixed = jax.random.permutation(jax.random.fold_in(own, 3), number_of)
    source_of, receiver = mixed[0:number_of // 2 * 2:2], mixed[1:number_of // 2 * 2:2]
    room = jnp.minimum(lengths[source_of] - 1, limit - lengths[receiver]) // 2
    room = jnp.where((source_of == order[0]) | (receiver == order[0]) | (lengths[receiver] == 0), 0, jnp.maximum(room, 0))
    passed = jax.random.randint(jax.random.fold_in(own, 4), (number_of // 2,), 0, 1 << 20) % (room + 1)
    lengths = lengths.at[source_of].add(-passed).at[receiver].add(passed)
    members = jnp.searchsorted(jnp.cumsum(lengths), jnp.arange(rows * top), side="right").astype(jnp.int32)
    table = members.reshape(top, rows).T
    table = table[jax.random.permutation(jax.random.fold_in(own, 1), rows)]
    turn = jax.random.randint(jax.random.fold_in(own, 2), (rows, 1), 0, top)
    return jnp.take_along_axis(table, (jnp.arange(top)[None, :] + turn) % top, axis=1)


def shares(amount, total, reach, slope, full):
    loads = [(1 << 20) // math.isqrt(rank ** slope) + 1 for rank in range(1, amount + 1)]
    largest = reach if full else min(reach, max(-(-total // amount), total * loads[0] // sum(loads)))
    least = 1 if total - largest >= amount - 1 else 0
    counts, rest = [largest] + [least] * (amount - 1), total - largest - least * (amount - 1)
    while rest > 0:
        movable = [i for i in range(1, amount) if counts[i] < largest] or [i for i in range(1, amount) if counts[i] < reach]
        pool, remaining = sum([loads[i] for i in movable]), rest
        for i in movable:
            more = min(reach - counts[i], max(1, remaining * loads[i] // pool), rest)
            counts[i] = counts[i] + more
            rest = rest - more
    return np.array(counts)


def gaussian(rng, extent, deviation, bound, pieces=(), kind=jnp.bfloat16):
    gain = levels(rng, extent, pieces, -0.22, 0.18) if pieces else 1.0
    result = jax.random.normal(rng, extent, jnp.float32) * deviation * gain
    return jnp.minimum(jnp.maximum(result, -bound), bound).astype(kind)


def setup_inputs(seed: int = 0) -> dict:
    splits = jax.random.split(jax.random.key(seed), 8)
    tokens = gaussian(splits[0], (TOKENS, D), 1.0, 6.0, ((0, 256), (1, 4)))
    cotangent = gaussian(splits[1], (TOKENS, D), 0.0625, 0.375, ((0, 256), (1, 4)))
    combine_weights = jnp.clip(0.19921875 + 0.80078125 * jax.random.uniform(splits[2], (TOKENS, TOP), jnp.float32) ** levels(splits[2], (TOKENS, TOP), ((0, 256),), -0.2, 0.2), 0.19921875, 1.0).astype(jnp.bfloat16)
    routes_keys = jax.random.split(jax.random.fold_in(splits[3], 1), TOKENS // TOK_DEV)
    routes_turns = jax.random.permutation(jax.random.fold_in(splits[3], 3), TOKENS // TOK_DEV)
    routes = jax.vmap(lambda own, number: assign_block(jax.random.fold_in(splits[3], 2), own, number, TOK_DEV, EXPERTS, TOP, CAP, 2))(routes_keys, routes_turns).reshape((TOKENS, TOP))
    w_gate = gaussian(splits[4], (EXPERTS, D, FF), D ** -0.5, 0.09375, ((0, 32), (1, 4)))
    w_up = gaussian(splits[5], (EXPERTS, D, FF), D ** -0.5, 0.09375, ((0, 32), (1, 4)))
    w_down = gaussian(splits[6], (EXPERTS, FF, D), FF ** -0.5, 0.21875, ((0, 32), (2, 4)))
    return dict(tokens=tokens, cotangent=cotangent, combine_weights=combine_weights, routes=routes, w_gate=w_gate, w_up=w_up, w_down=w_down)


def rounded(value):
    return lax.optimization_barrier(value.astype(jnp.bfloat16)).astype(jnp.float32)


def select_rows(table_rows, row_ids):
    return table_rows[row_ids]


def reference(tokens, cotangent, combine_weights, routes, w_gate, w_up, w_down):
    block_count = N_DP * N_CTX
    quarter_dim = D // N_TP
    route_count = TOK_DEV * TOP
    group_rows = N_CTX * CAP
    route_ids = routes.reshape(block_count, route_count)
    one_hot = (route_ids[:, :, None] == jnp.arange(EXPERTS, dtype=jnp.int32)[None, None, :]).astype(jnp.int32)
    slot_ids = jnp.sum(one_hot * jnp.cumsum(one_hot, axis=1), axis=2) - 1
    block_ids = jnp.broadcast_to(jnp.arange(block_count, dtype=jnp.int32)[:, None], (block_count, route_count))
    row_tokens = jnp.broadcast_to((jnp.arange(route_count, dtype=jnp.int32) // TOP)[None, :], (block_count, route_count))
    token_of = jnp.full((block_count, EXPERTS, CAP), TOK_DEV, jnp.int32).at[block_ids, route_ids, slot_ids].set(row_tokens)
    weight_of = jnp.zeros((block_count, EXPERTS, CAP), jnp.bfloat16).at[block_ids, route_ids, slot_ids].set(combine_weights.reshape(block_count, route_count))
    pad_rows = jnp.zeros((block_count, 1, D), jnp.bfloat16)
    token_table = jnp.concatenate([tokens.reshape(block_count, TOK_DEV, D), pad_rows], axis=1)
    cot_table = jnp.concatenate([cotangent.reshape(block_count, TOK_DEV, D), pad_rows], axis=1)

    def expert(operands):
        slot_token, slot_weight, gate_mat, up_mat, down_mat = operands
        rows_in = jax.vmap(select_rows)(token_table, slot_token).reshape(N_DP, group_rows, D)
        cot_in = jax.vmap(select_rows)(cot_table, slot_token).reshape(N_DP, group_rows, D)
        rows_quarters = rows_in.astype(jnp.float32).reshape(N_DP, group_rows, N_TP, quarter_dim)
        cot_quarters = cot_in.astype(jnp.float32).reshape(N_DP, group_rows, N_TP, quarter_dim)
        gate_quarters = gate_mat.astype(jnp.float32).reshape(N_TP, quarter_dim, FF)
        up_quarters = up_mat.astype(jnp.float32).reshape(N_TP, quarter_dim, FF)
        down_quarters = down_mat.astype(jnp.float32).reshape(FF, N_TP, quarter_dim)
        pre_gate = jnp.sum(rounded(jnp.einsum('grqd,qdf->grqf', rows_quarters, gate_quarters)), axis=2)
        pre_up = jnp.sum(rounded(jnp.einsum('grqd,qdf->grqf', rows_quarters, up_quarters)), axis=2)
        back_grad = jnp.sum(rounded(jnp.einsum('grqd,fqd->grqf', cot_quarters, down_quarters)), axis=2)
        sig_gate = jax.nn.sigmoid(pre_gate)
        silu_gate = pre_gate * sig_gate
        hidden = (silu_gate * pre_up).astype(jnp.bfloat16)
        hidden_wide = hidden.astype(jnp.float32)
        out_rows = jnp.einsum('grf,fd->grd', hidden_wide, down_mat.astype(jnp.float32)).astype(jnp.bfloat16)
        slot_grads = jnp.sum(hidden_wide * back_grad, axis=2).astype(jnp.bfloat16)
        d_hidden = slot_weight.reshape(N_DP, group_rows, 1).astype(jnp.float32) * back_grad
        d_up = (d_hidden * silu_gate).astype(jnp.bfloat16)
        d_gate = (d_hidden * pre_up * sig_gate * (1.0 + pre_gate * (1.0 - sig_gate))).astype(jnp.bfloat16)
        rows_wide = rows_in.astype(jnp.float32)
        grad_gate = jnp.sum(rounded(jnp.einsum('grd,grf->gdf', rows_wide, d_gate.astype(jnp.float32))), axis=0)
        grad_up = jnp.sum(rounded(jnp.einsum('grd,grf->gdf', rows_wide, d_up.astype(jnp.float32))), axis=0)
        return out_rows.reshape(block_count, CAP, D), slot_grads.reshape(block_count, CAP), grad_gate, grad_up

    out_rows, slot_grads, grad_gate, grad_up = lax.map(expert, (jnp.transpose(token_of, (1, 0, 2)), jnp.transpose(weight_of, (1, 0, 2)), w_gate, w_up, w_down))
    picked = out_rows[route_ids, block_ids, slot_ids].reshape(block_count * TOK_DEV, TOP, D)
    scales = combine_weights.astype(jnp.float32)[:, :, None]
    mixed = jnp.sum(scales * picked.astype(jnp.float32), axis=1).astype(jnp.bfloat16)
    combine_grads = slot_grads[route_ids, block_ids, slot_ids].reshape(block_count * TOK_DEV, TOP)
    return mixed, combine_grads, grad_gate, grad_up
```

```python
import functools

import jax
import jax.numpy as jnp
from jax import lax
from jax.experimental import pallas as pl
from jax.experimental.pallas import tpu as pltpu
from jax.sharding import PartitionSpec as P

LANES = 128
VMEM_LIMIT = 16 * 1024 * 1024
ROWS_0 = (((0,), (0,)), ((), ()))
PLAIN = (((1,), (0,)), ((), ()))
TURNED = (((1,), (1,)), ((), ()))
ANYWHERE = pl.BlockSpec(memory_space=pl.ANY)
IN_VMEM = pl.BlockSpec(memory_space=pltpu.VMEM)


def product(left, right, dims=PLAIN):
    return lax.dot_general(left, right, dims, preferred_element_type=jnp.float32)


def exchange(blocks, axis):
    return lax.all_to_all(blocks, axis, split_axis=0, concat_axis=0, tiled=True)


def swap(value, bit):
    perm = [(i, i ^ bit) for i in range(lax.axis_size("tp"))]
    return lax.ppermute(value, "tp", perm)


def in_hbm(value):
    return pltpu.with_memory_space_constraint(value, pltpu.HBM)


def pallas(body, out_shape, **given):
    return pl.pallas_call(
        body,
        out_shape=out_shape,
        compiler_params=pltpu.CompilerParams(vmem_limit_bytes=VMEM_LIMIT),
        cost_estimate=pl.CostEstimate(flops=0, bytes_accessed=0, transcendentals=0),
        **given,
    )


def tie(value, *behind):
    return pallas(
        lambda *refs: None,
        jax.ShapeDtypeStruct(value.shape, value.dtype),
        in_specs=[ANYWHERE] * (1 + len(behind)),
        out_specs=ANYWHERE,
        input_output_aliases={0: 0},
    )(value, *behind)


def as_blocks(flat):
    rows, width = flat.shape
    return flat.reshape(rows, width // LANES, LANES).reshape(-1, LANES)


def as_rows(blocks, width):
    return blocks.reshape(-1, width // LANES, LANES).reshape(-1, width)


def slot_maps(routes, experts, capacity):
    top_count, tok_count = routes.shape
    names = [routes[k : k + 1, :] for k in range(top_count)]
    expert_ids = lax.broadcasted_iota(jnp.int32, (experts, tok_count), 0)
    named = [expert_ids == name for name in names]
    both = sum(one.astype(jnp.float32) for one in named).astype(jnp.bfloat16)
    earlier = lax.broadcasted_iota(jnp.int32, (tok_count, tok_count), 0)
    later = lax.broadcasted_iota(jnp.int32, (tok_count, tok_count), 1)
    counts = product(both, (earlier < later).astype(jnp.float32).astype(jnp.bfloat16))
    slot_rows = lax.broadcasted_iota(jnp.int32, (experts * capacity, tok_count), 0)
    maps = []
    for name, one in zip(names, named):
        slots = jnp.sum(jnp.where(one, counts, 0.0), axis=0, keepdims=True)
        maps.append(slot_rows == name * capacity + slots.astype(jnp.int32))
    return maps


def weighted_map(maps, scales):
    total = 0.0
    for k, one in enumerate(maps):
        total = total + jnp.where(one, 1.0 if scales is None else scales[k : k + 1, :], 0.0)
    return total.astype(jnp.bfloat16)


def dispatch_kernel(experts, capacity, routes_ref, scale_ref, tok_ref, cot_ref, x_ref, c_ref):
    maps = slot_maps(routes_ref[...], experts, capacity)
    scales = scale_ref[...].astype(jnp.float32)
    for out_ref, source_ref, given in ((x_ref, tok_ref, None), (c_ref, cot_ref, scales)):
        picked = product(weighted_map(maps, given), source_ref[...])
        out_ref[...] = as_blocks(picked).astype(jnp.bfloat16)


def combine_kernel(experts, capacity, routes_ref, scale_ref, back_ref, cot_ref, mixed_ref, dots_ref):
    maps = slot_maps(routes_ref[...], experts, capacity)
    scales = scale_ref[...].astype(jnp.float32)
    back = as_rows(back_ref[...], cot_ref.shape[1])
    mixed_ref[...] = product(weighted_map(maps, scales), back, ROWS_0).astype(jnp.bfloat16)
    meets = product(back, cot_ref[...], TURNED)
    for k, one in enumerate(maps):
        dots_ref[k : k + 1, :] = jnp.sum(jnp.where(one, meets, 0.0), axis=0, keepdims=True)


def split_halves(total, core):
    half = total.shape[0] // 2
    first, second = total[:half], total[half:]
    return jnp.where(core == 0, first, second), jnp.where(core == 0, second, first)


def pre_kernel(place_ref, x_ref, gate_ref, up_ref, mine_ref, theirs_ref, rows_ref):
    @pl.when(pl.program_id(0) == 0)
    def _():
        rows_ref[...] = as_rows(x_ref[...], rows_ref.shape[1])

    for k, w_ref in enumerate((gate_ref, up_ref)):
        mine, theirs = split_halves(product(rows_ref[...], w_ref[0]), place_ref[0])
        mine_ref[k] = mine
        theirs_ref[k] = theirs.astype(jnp.bfloat16)


def pre_products(place, x_blocks, w_gate, w_up):
    _, depth, width = w_gate.shape
    rows = x_blocks.size // depth
    half, step = rows // 2, width // 3
    w_spec = pl.BlockSpec((1, depth, step), lambda i, place: (0, 0, i))
    out_spec = pl.BlockSpec((2, half, step), lambda i, place: (0, 0, i))
    return pallas(
        pre_kernel,
        (
            jax.ShapeDtypeStruct((2, half, width), jnp.float32),
            jax.ShapeDtypeStruct((2, half, width), jnp.bfloat16),
            jax.ShapeDtypeStruct((rows, depth), jnp.bfloat16),
        ),
        grid_spec=pltpu.PrefetchScalarGridSpec(
            num_scalar_prefetch=1,
            grid=(3,),
            in_specs=[pl.BlockSpec(x_blocks.shape, lambda i, place: (0, 0)), w_spec, w_spec],
            out_specs=(out_spec, out_spec, pl.BlockSpec((rows, depth), lambda i, place: (0, 0))),
        ),
    )(place, x_blocks, in_hbm(w_gate), in_hbm(w_up))


def slope_kernel(place_ref, cot_ref, w_ref, _, mine_ref, theirs_ref):
    total = product(as_rows(cot_ref[...], w_ref.shape[2]), w_ref[0], TURNED)
    mine, theirs = split_halves(total, place_ref[0])
    mine_ref[...] = mine
    theirs_ref[...] = theirs.astype(jnp.bfloat16)


def slope_products(place, cot_blocks, w_down, behind):
    half = cot_blocks.size // w_down.shape[2] // 2
    shape = (half, w_down.shape[1])
    return pallas(
        slope_kernel,
        (jax.ShapeDtypeStruct(shape, jnp.float32), jax.ShapeDtypeStruct(shape, jnp.bfloat16)),
        in_specs=[pl.BlockSpec(memory_space=pltpu.SMEM), IN_VMEM, IN_VMEM, ANYWHERE],
        out_specs=(IN_VMEM, IN_VMEM),
    )(place, cot_blocks, w_down, behind)


def gated(pre_ref, pre_got_ref):
    pre_gate = pre_ref[0].astype(jnp.float32) + pre_got_ref[0].astype(jnp.float32)
    pre_up = pre_ref[1].astype(jnp.float32) + pre_got_ref[1].astype(jnp.float32)
    return pre_gate, pre_up, jax.nn.sigmoid(pre_gate)


def hidden_kernel(pre_ref, pre_got_ref, out_ref):
    pre_gate, pre_up, sig_gate = gated(pre_ref, pre_got_ref)
    out_ref[...] = (pre_gate * sig_gate * pre_up).astype(jnp.bfloat16)


def out_kernel(place_ref, own_ref, other_ref, w_ref, out_ref):
    own, other = own_ref[...], other_ref[...]
    core = place_ref[0]
    hidden = jnp.concatenate(
        [jnp.where(core == 0, own, other), jnp.where(core == 0, other, own)], axis=0
    )
    out_ref[...] = as_blocks(product(hidden, w_ref[0])).astype(jnp.bfloat16)


def out_products(place, own, other, w_down):
    size = 2 * own.shape[0] * w_down.shape[2]
    return pallas(
        out_kernel,
        jax.ShapeDtypeStruct((size // LANES, LANES), jnp.bfloat16),
        in_specs=[pl.BlockSpec(memory_space=pltpu.SMEM), IN_VMEM, IN_VMEM, IN_VMEM],
        out_specs=IN_VMEM,
    )(place, own, other, w_down)


def slopes_kernel(groups, pre_ref, pre_got_ref, slope_ref, slope_got_ref, _, out_ref):
    pre_gate, pre_up, sig_gate = gated(pre_ref, pre_got_ref)
    d_hidden = slope_ref[...].astype(jnp.float32) + slope_got_ref[...].astype(jnp.float32)
    d_up = d_hidden * (pre_gate * sig_gate)
    d_gate = d_hidden * pre_up * sig_gate * (1.0 + pre_gate * (1.0 - sig_gate))
    half, width = d_up.shape
    fold, part = half // 2, width // groups
    for j in range(groups):
        cols = slice(j * part, (j + 1) * part)
        chunk = jnp.concatenate(
            [d_gate[:fold, cols], d_up[:fold, cols], d_gate[fold:, cols], d_up[fold:, cols]],
            axis=1,
        )
        out_ref[j] = chunk.astype(jnp.bfloat16)


def slopes(pre, pre_got, slope, slope_got, behind, groups):
    half, width = slope.shape
    return pallas(
        functools.partial(slopes_kernel, groups),
        jax.ShapeDtypeStruct((groups, half // 2, 4 * width // groups), jnp.bfloat16),
        in_specs=[IN_VMEM] * 4 + [ANYWHERE],
        out_specs=IN_VMEM,
    )(pre, pre_got, slope, slope_got, behind)


def grads_kernel(with_add, _, x_ref, d_ref, *refs):
    gate_ref, up_ref = refs[-2:]
    count, _, half, width = x_ref.shape
    part = gate_ref.shape[0]
    folds = []
    for g in range(count):
        folds += [d_ref[g][:, : 2 * part], d_ref[g][:, 2 * part :]]
    rows = x_ref[...].reshape(count * half, width)
    total = product(jnp.concatenate(folds, axis=0), rows, ROWS_0)
    first = pl.program_id(0) == 0
    for k, out_ref in enumerate((gate_ref, up_ref)):
        before = jnp.where(first, refs[k][...] if with_add else 0.0, out_ref[...])
        out_ref[...] = before + total[k * part : (k + 1) * part]


def weight_grads(place, own, x_all, d_got, add=()):
    groups, _, half, width = x_all.shape
    _, fold, packed = d_got.shape
    part = packed // 4
    count = groups // 2
    out_spec = pl.BlockSpec((part, width), lambda i, place: (0, 0))
    return pallas(
        functools.partial(grads_kernel, bool(add)),
        (jax.ShapeDtypeStruct((part, width), jnp.float32),) * 2,
        grid_spec=pltpu.PrefetchScalarGridSpec(
            num_scalar_prefetch=1,
            grid=(2,),
            in_specs=[
                pl.BlockSpec(
                    (count, 1, half, width),
                    lambda i, place: (i, place[0] if own else 1 - place[0], 0, 0),
                ),
                pl.BlockSpec((count, fold, packed), lambda i, place: (i, 0, 0)),
            ]
            + [out_spec] * len(add),
            out_specs=(out_spec, out_spec),
        ),
    )(place, in_hbm(x_all), d_got, *add)


def shards(tokens, cotangent, combine_weights, routes, w_gate, w_up, w_down):
    experts = lax.axis_size("ctx")
    groups = lax.axis_size("dp")
    tok_count, top_count = routes.shape
    quarter = tokens.shape[1]
    capacity = 5 * tok_count * top_count // (4 * experts)
    rows = experts * capacity
    place = (lax.axis_index("tp") % 2).astype(jnp.int32)[None]
    blocks = jax.ShapeDtypeStruct((rows * quarter // LANES, LANES), jnp.bfloat16)

    def over_ctx(flat):
        return exchange(flat.reshape(experts, -1, LANES), "ctx").reshape(flat.shape)

    routes_t, weights_t = routes.T, combine_weights.T
    x_send, cot_send = pallas(
        functools.partial(dispatch_kernel, experts, capacity), (blocks, blocks)
    )(routes_t, weights_t, in_hbm(tokens), in_hbm(cotangent))
    x_got = over_ctx(x_send)
    cot_got = over_ctx(cot_send)

    pre_mine, pre_theirs, x_rows = pre_products(place, x_got, w_gate, w_up)
    x_all = lax.all_gather(x_rows, "dp", axis=0, tiled=True)
    pre = (pre_mine + swap(pre_theirs, 1).astype(jnp.float32)).astype(jnp.bfloat16)
    pre_got = swap(pre, 2)
    hidden = pallas(hidden_kernel, jax.ShapeDtypeStruct(pre.shape[1:], jnp.bfloat16))(pre, pre_got)
    out_send = out_products(place, hidden, swap(hidden, 1), w_down)
    out_got = over_ctx(out_send)

    slope_mine, slope_theirs = slope_products(place, cot_got, w_down, out_send)
    slope = (slope_mine + swap(slope_theirs, 1).astype(jnp.float32)).astype(jnp.bfloat16)
    d_got = exchange(slopes(pre, pre_got, slope, swap(slope, 2), out_got, groups), "dp")

    mixed, dots = pallas(
        functools.partial(combine_kernel, experts, capacity),
        (
            jax.ShapeDtypeStruct(tokens.shape, jnp.bfloat16),
            jax.ShapeDtypeStruct(routes_t.shape, jnp.float32),
        ),
    )(routes_t, weights_t, out_got, in_hbm(cotangent))
    dots = dots + swap(dots, 1)
    dots = dots + swap(dots, 2)
    combine_grads = dots.T.astype(jnp.bfloat16)

    d_got = tie(d_got, dots)
    x_all = x_all.reshape(groups, 2, rows // 2, quarter)
    part_grads = weight_grads(place, True, x_all, d_got)
    grad_gate, grad_up = weight_grads(place, False, x_all, swap(d_got, 1), part_grads)
    return (mixed, combine_grads, grad_gate.T[None], grad_up.T[None])


def solution(mesh):
    in_specs = (
        P(("dp", "ctx"), "tp"),
        P(("dp", "ctx"), "tp"),
        P(("dp", "ctx"), None),
        P(("dp", "ctx"), None),
        P("ctx", "tp", None),
        P("ctx", "tp", None),
        P("ctx", None, "tp"),
    )
    out_specs = (
        P(("dp", "ctx"), "tp"),
        P(("dp", "ctx"), None),
        P("ctx", "tp", "dp"),
        P("ctx", "tp", "dp"),
    )
    return jax.shard_map(shards, mesh=mesh, in_specs=in_specs, out_specs=out_specs, check_vma=False)
```

```python
import functools

import jax
import jax.numpy as jnp
from jax import lax
from jax.experimental import pallas as pl
from jax.experimental.pallas import tpu as pltpu
from jax.sharding import PartitionSpec as P

LANES = 128
VMEM_LIMIT = 16 * 1024 * 1024
ROWS_0 = (((0,), (0,)), ((), ()))
PLAIN = (((1,), (0,)), ((), ()))
TURNED = (((1,), (1,)), ((), ()))
ANYWHERE = pl.BlockSpec(memory_space=pl.ANY)
IN_VMEM = pl.BlockSpec(memory_space=pltpu.VMEM)


def product(left, right, dims=PLAIN):
    return lax.dot_general(left, right, dims, preferred_element_type=jnp.float32)


def exchange(blocks, axis):
    return lax.all_to_all(blocks, axis, split_axis=0, concat_axis=0, tiled=True)


def swap(value, bit):
    perm = [(i, i ^ bit) for i in range(lax.axis_size("tp"))]
    return lax.ppermute(value, "tp", perm)


def in_hbm(value):
    return pltpu.with_memory_space_constraint(value, pltpu.HBM)


def pallas(body, out_shape, **given):
    return pl.pallas_call(
        body,
        out_shape=out_shape,
        compiler_params=pltpu.CompilerParams(vmem_limit_bytes=VMEM_LIMIT),
        cost_estimate=pl.CostEstimate(flops=0, bytes_accessed=0, transcendentals=0),
        **given,
    )


def tie(value, *behind):
    return pallas(
        lambda *refs: None,
        jax.ShapeDtypeStruct(value.shape, value.dtype),
        in_specs=[ANYWHERE] * (1 + len(behind)),
        out_specs=ANYWHERE,
        input_output_aliases={0: 0},
    )(value, *behind)


def as_blocks(flat):
    rows, width = flat.shape
    return flat.reshape(rows, width // LANES, LANES).reshape(-1, LANES)


def as_rows(blocks, width):
    return blocks.reshape(-1, width // LANES, LANES).reshape(-1, width)


def slot_maps(routes, experts, capacity):
    top_count, tok_count = routes.shape
    names = [routes[k : k + 1, :] for k in range(top_count)]
    expert_ids = lax.broadcasted_iota(jnp.int32, (experts, tok_count), 0)
    named = [expert_ids == name for name in names]
    both = sum(one.astype(jnp.float32) for one in named).astype(jnp.bfloat16)
    earlier = lax.broadcasted_iota(jnp.int32, (tok_count, tok_count), 0)
    later = lax.broadcasted_iota(jnp.int32, (tok_count, tok_count), 1)
    counts = product(both, (earlier < later).astype(jnp.float32).astype(jnp.bfloat16))
    slot_rows = lax.broadcasted_iota(jnp.int32, (experts * capacity, tok_count), 0)
    maps = []
    for name, one in zip(names, named):
        slots = jnp.sum(jnp.where(one, counts, 0.0), axis=0, keepdims=True)
        maps.append(slot_rows == name * capacity + slots.astype(jnp.int32))
    return maps


def weighted_map(maps, scales):
    total = 0.0
    for k, one in enumerate(maps):
        total = total + jnp.where(one, 1.0 if scales is None else scales[k : k + 1, :], 0.0)
    return total.astype(jnp.bfloat16)


def dispatch_kernel(experts, capacity, routes_ref, *refs):
    scale_refs, (source_ref, out_ref) = refs[:-2], refs[-2:]
    maps = slot_maps(routes_ref[...], experts, capacity)
    scales = scale_refs[0][...].astype(jnp.float32) if scale_refs else None
    picked = product(weighted_map(maps, scales), source_ref[...])
    out_ref[...] = as_blocks(picked).astype(jnp.bfloat16)


def combine_kernel(experts, capacity, routes_ref, scale_ref, back_ref, cot_ref, mixed_ref, dots_ref):
    maps = slot_maps(routes_ref[...], experts, capacity)
    scales = scale_ref[...].astype(jnp.float32)
    back = as_rows(back_ref[...], cot_ref.shape[1])
    mixed_ref[...] = product(weighted_map(maps, scales), back, ROWS_0).astype(jnp.bfloat16)
    meets = product(back, cot_ref[...], TURNED)
    for k, one in enumerate(maps):
        dots_ref[k : k + 1, :] = jnp.sum(jnp.where(one, meets, 0.0), axis=0, keepdims=True)


def split_halves(total, core):
    half = total.shape[0] // 2
    first, second = total[:half], total[half:]
    return jnp.where(core == 0, first, second), jnp.where(core == 0, second, first)


def pre_kernel(place_ref, x_ref, gate_ref, up_ref, _, mine_ref, theirs_ref, rows_ref):
    @pl.when(pl.program_id(0) == 0)
    def _():
        rows_ref[...] = as_rows(x_ref[...], rows_ref.shape[1])

    for k, w_ref in enumerate((gate_ref, up_ref)):
        mine, theirs = split_halves(product(rows_ref[...], w_ref[0]), place_ref[0])
        mine_ref[k] = mine.astype(jnp.bfloat16)
        theirs_ref[k] = theirs.astype(jnp.bfloat16)


def pre_products(place, x_blocks, w_gate, w_up, behind):
    _, depth, width = w_gate.shape
    rows = x_blocks.size // depth
    half, step = rows // 2, width // 3
    w_spec = pl.BlockSpec((1, depth, step), lambda i, place: (0, 0, i))
    out_spec = pl.BlockSpec((2, half, step), lambda i, place: (0, 0, i))
    return pallas(
        pre_kernel,
        (
            jax.ShapeDtypeStruct((2, half, width), jnp.bfloat16),
            jax.ShapeDtypeStruct((2, half, width), jnp.bfloat16),
            jax.ShapeDtypeStruct((rows, depth), jnp.bfloat16),
        ),
        grid_spec=pltpu.PrefetchScalarGridSpec(
            num_scalar_prefetch=1,
            grid=(3,),
            in_specs=[
                pl.BlockSpec(x_blocks.shape, lambda i, place: (0, 0)),
                w_spec,
                w_spec,
                ANYWHERE,
            ],
            out_specs=(out_spec, out_spec, pl.BlockSpec((rows, depth), lambda i, place: (0, 0))),
        ),
    )(place, x_blocks, in_hbm(w_gate), in_hbm(w_up), behind)


def slope_kernel(place_ref, cot_ref, w_ref, _, mine_ref, theirs_ref):
    total = product(as_rows(cot_ref[...], w_ref.shape[2]), w_ref[0], TURNED)
    mine, theirs = split_halves(total, place_ref[0])
    mine_ref[...] = mine.astype(jnp.bfloat16)
    theirs_ref[...] = theirs.astype(jnp.bfloat16)


def slope_products(place, cot_blocks, w_down, behind):
    half = cot_blocks.size // w_down.shape[2] // 2
    shape = (half, w_down.shape[1])
    return pallas(
        slope_kernel,
        (jax.ShapeDtypeStruct(shape, jnp.bfloat16),) * 2,
        in_specs=[pl.BlockSpec(memory_space=pltpu.SMEM), IN_VMEM, IN_VMEM, ANYWHERE],
        out_specs=(IN_VMEM, IN_VMEM),
    )(place, cot_blocks, w_down, behind)


def chip_sum_kernel(mine_ref, got_ref, out_ref):
    total = mine_ref[...].astype(jnp.float32) + got_ref[...].astype(jnp.float32)
    out_ref[...] = total.astype(jnp.bfloat16)


def chip_sum(mine, got):
    return pallas(
        chip_sum_kernel,
        jax.ShapeDtypeStruct(got.shape, got.dtype),
        in_specs=[IN_VMEM, IN_VMEM],
        out_specs=IN_VMEM,
    )(mine, got)


def gated(pre_ref, pre_got_ref):
    pre_gate = pre_ref[0].astype(jnp.float32) + pre_got_ref[0].astype(jnp.float32)
    pre_up = pre_ref[1].astype(jnp.float32) + pre_got_ref[1].astype(jnp.float32)
    return pre_gate, pre_up, jax.nn.sigmoid(pre_gate)


def hidden_kernel(pre_ref, pre_got_ref, _, out_ref):
    pre_gate, pre_up, sig_gate = gated(pre_ref, pre_got_ref)
    out_ref[...] = (pre_gate * sig_gate * pre_up).astype(jnp.bfloat16)


def out_kernel(place_ref, own_ref, other_ref, w_ref, _, out_ref):
    own, other = own_ref[...], other_ref[...]
    core = place_ref[0]
    hidden = jnp.concatenate(
        [jnp.where(core == 0, own, other), jnp.where(core == 0, other, own)], axis=0
    )
    out_ref[...] = as_blocks(product(hidden, w_ref[0])).astype(jnp.bfloat16)


def out_products(place, own, other, w_down, behind):
    size = 2 * own.shape[0] * w_down.shape[2]
    return pallas(
        out_kernel,
        jax.ShapeDtypeStruct((size // LANES, LANES), jnp.bfloat16),
        in_specs=[pl.BlockSpec(memory_space=pltpu.SMEM), IN_VMEM, IN_VMEM, IN_VMEM, ANYWHERE],
        out_specs=IN_VMEM,
    )(place, own, other, w_down, behind)


def slopes_kernel(groups, pre_ref, pre_got_ref, slope_ref, slope_got_ref, out_ref):
    pre_gate, pre_up, sig_gate = gated(pre_ref, pre_got_ref)
    d_hidden = slope_ref[...].astype(jnp.float32) + slope_got_ref[...].astype(jnp.float32)
    d_up = d_hidden * (pre_gate * sig_gate)
    d_gate = d_hidden * pre_up * sig_gate * (1.0 + pre_gate * (1.0 - sig_gate))
    half, width = d_up.shape
    fold, part = half // 2, width // groups
    for j in range(groups):
        cols = slice(j * part, (j + 1) * part)
        chunk = jnp.concatenate(
            [d_gate[:fold, cols], d_up[:fold, cols], d_gate[fold:, cols], d_up[fold:, cols]],
            axis=1,
        )
        out_ref[j] = chunk.astype(jnp.bfloat16)


def slopes(pre, pre_got, slope, slope_got, groups):
    half, width = slope.shape
    return pallas(
        functools.partial(slopes_kernel, groups),
        jax.ShapeDtypeStruct((groups, half // 2, 4 * width // groups), jnp.bfloat16),
        in_specs=[IN_VMEM] * 4,
        out_specs=IN_VMEM,
    )(pre, pre_got, slope, slope_got)


def grads_kernel(with_add, _, x_ref, d_ref, *refs):
    gate_ref, up_ref = refs[-2:]
    count, _, half, width = x_ref.shape
    part = gate_ref.shape[0]
    folds = []
    for g in range(count):
        folds += [d_ref[g][:, : 2 * part], d_ref[g][:, 2 * part :]]
    rows = x_ref[...].reshape(count * half, width)
    total = product(jnp.concatenate(folds, axis=0), rows, ROWS_0)
    first = pl.program_id(0) == 0
    for k, out_ref in enumerate((gate_ref, up_ref)):
        before = jnp.where(first, refs[k][...] if with_add else 0.0, out_ref[...])
        out_ref[...] = before + total[k * part : (k + 1) * part]


def weight_grads(place, own, x_all, d_got, add=()):
    groups, _, half, width = x_all.shape
    _, fold, packed = d_got.shape
    part = packed // 4
    count = groups // 2
    out_spec = pl.BlockSpec((part, width), lambda i, place: (0, 0))
    return pallas(
        functools.partial(grads_kernel, bool(add)),
        (jax.ShapeDtypeStruct((part, width), jnp.float32),) * 2,
        grid_spec=pltpu.PrefetchScalarGridSpec(
            num_scalar_prefetch=1,
            grid=(2,),
            in_specs=[
                pl.BlockSpec(
                    (count, 1, half, width),
                    lambda i, place: (i, place[0] if own else 1 - place[0], 0, 0),
                ),
                pl.BlockSpec((count, fold, packed), lambda i, place: (i, 0, 0)),
            ]
            + [out_spec] * len(add),
            out_specs=(out_spec, out_spec),
        ),
    )(place, in_hbm(x_all), d_got, *add)


def shards(tokens, cotangent, combine_weights, routes, w_gate, w_up, w_down):
    experts = lax.axis_size("ctx")
    groups = lax.axis_size("dp")
    tok_count, top_count = routes.shape
    quarter = tokens.shape[1]
    capacity = 5 * tok_count * top_count // (4 * experts)
    rows = experts * capacity
    place = (lax.axis_index("tp") % 2).astype(jnp.int32)[None]
    blocks = jax.ShapeDtypeStruct((rows * quarter // LANES, LANES), jnp.bfloat16)

    def over_ctx(flat):
        return exchange(flat.reshape(experts, -1, LANES), "ctx").reshape(flat.shape)

    routes_t, weights_t = in_hbm(routes.T), in_hbm(combine_weights.T)
    dispatch = pallas(functools.partial(dispatch_kernel, experts, capacity), blocks)
    x_got = over_ctx(dispatch(routes_t, in_hbm(tokens)))
    cot_send = dispatch(routes_t, weights_t, in_hbm(cotangent))
    cot_got = over_ctx(cot_send)

    pre_mine, pre_theirs, x_rows = pre_products(place, x_got, w_gate, w_up, cot_send)
    x_all = lax.all_gather(x_rows, "dp", axis=0, tiled=True)
    pre = chip_sum(pre_mine, swap(pre_theirs, 1))
    pre_got = swap(pre, 2)
    hidden = pallas(
        hidden_kernel,
        jax.ShapeDtypeStruct(pre.shape[1:], jnp.bfloat16),
        in_specs=[IN_VMEM, IN_VMEM, ANYWHERE],
        out_specs=IN_VMEM,
    )(pre, pre_got, cot_got)
    slope_mine, slope_theirs = slope_products(place, cot_got, w_down, hidden)
    slope_swapped = swap(slope_theirs, 1)
    out_send = out_products(place, hidden, swap(hidden, 1), w_down, slope_theirs)
    out_got = over_ctx(out_send)
    slope = chip_sum(slope_mine, slope_swapped)
    slope_got = swap(slope, 2)
    d_send = slopes(pre, pre_got, slope, slope_got, groups)
    d_got = exchange(tie(d_send, out_got), "dp")

    mixed, dots = pallas(
        functools.partial(combine_kernel, experts, capacity),
        (
            jax.ShapeDtypeStruct(tokens.shape, jnp.bfloat16),
            jax.ShapeDtypeStruct(routes_t.shape, jnp.float32),
        ),
    )(routes_t, weights_t, out_got, in_hbm(cotangent))
    dots = dots + swap(dots, 1)
    dots = dots + swap(dots, 2)
    combine_grads = dots.T.astype(jnp.bfloat16)

    d_got = tie(d_got, dots)
    x_all = x_all.reshape(groups, 2, rows // 2, quarter)
    part_grads = weight_grads(place, True, x_all, d_got)
    grad_gate, grad_up = weight_grads(place, False, x_all, swap(d_got, 1), part_grads)
    return (mixed, combine_grads, grad_gate.T[None], grad_up.T[None])


def solution(mesh):
    in_specs = (
        P(("dp", "ctx"), "tp"),
        P(("dp", "ctx"), "tp"),
        P(("dp", "ctx"), None),
        P(("dp", "ctx"), None),
        P("ctx", "tp", None),
        P("ctx", "tp", None),
        P("ctx", None, "tp"),
    )
    out_specs = (
        P(("dp", "ctx"), "tp"),
        P(("dp", "ctx"), None),
        P("ctx", "tp", "dp"),
        P("ctx", "tp", "dp"),
    )
    return jax.shard_map(shards, mesh=mesh, in_specs=in_specs, out_specs=out_specs, check_vma=False)
```

```python
import functools

import jax
import jax.numpy as jnp
from jax import lax
from jax.experimental import pallas as pl
from jax.experimental.pallas import tpu as pltpu
from jax.sharding import PartitionSpec as P

LANES = 128
VMEM_LIMIT = 16 * 1024 * 1024
ROWS_0 = (((0,), (0,)), ((), ()))
PLAIN = (((1,), (0,)), ((), ()))
TURNED = (((1,), (1,)), ((), ()))
ANYWHERE = pl.BlockSpec(memory_space=pl.ANY)
IN_VMEM = pl.BlockSpec(memory_space=pltpu.VMEM)


def product(left, right, dims=PLAIN):
    return lax.dot_general(left, right, dims, preferred_element_type=jnp.float32)


def exchange(blocks, axis):
    return lax.all_to_all(blocks, axis, split_axis=0, concat_axis=0, tiled=True)


def swap(value, bit):
    perm = [(i, i ^ bit) for i in range(lax.axis_size("tp"))]
    return lax.ppermute(value, "tp", perm)


def shift(value, places):
    groups = lax.axis_size("dp")
    return lax.ppermute(value, "dp", [(i, (i + places) % groups) for i in range(groups)])


def in_hbm(value):
    return pltpu.with_memory_space_constraint(value, pltpu.HBM)


def pallas(body, out_shape, **given):
    return pl.pallas_call(
        body,
        out_shape=out_shape,
        compiler_params=pltpu.CompilerParams(vmem_limit_bytes=VMEM_LIMIT),
        cost_estimate=pl.CostEstimate(flops=0, bytes_accessed=0, transcendentals=0),
        **given,
    )


def tie(value, *behind):
    return pallas(
        lambda *refs: None,
        jax.ShapeDtypeStruct(value.shape, value.dtype),
        in_specs=[ANYWHERE] * (1 + len(behind)),
        out_specs=ANYWHERE,
        input_output_aliases={0: 0},
    )(value, *behind)


def as_blocks(flat):
    rows, width = flat.shape
    return flat.reshape(rows, width // LANES, LANES).reshape(-1, LANES)


def as_rows(blocks, width):
    return blocks.reshape(-1, width // LANES, LANES).reshape(-1, width)


def slot_maps(routes, experts, capacity):
    top_count, tok_count = routes.shape
    names = [routes[k : k + 1, :] for k in range(top_count)]
    expert_ids = lax.broadcasted_iota(jnp.int32, (experts, tok_count), 0)
    named = [expert_ids == name for name in names]
    both = sum(one.astype(jnp.float32) for one in named).astype(jnp.bfloat16)
    earlier = lax.broadcasted_iota(jnp.int32, (tok_count, tok_count), 0)
    later = lax.broadcasted_iota(jnp.int32, (tok_count, tok_count), 1)
    counts = product(both, (earlier < later).astype(jnp.float32).astype(jnp.bfloat16))
    slot_rows = lax.broadcasted_iota(jnp.int32, (experts * capacity, tok_count), 0)
    maps = []
    for name, one in zip(names, named):
        slots = jnp.sum(jnp.where(one, counts, 0.0), axis=0, keepdims=True)
        maps.append(slot_rows == name * capacity + slots.astype(jnp.int32))
    return maps


def weighted_map(maps, scales):
    total = 0.0
    for k, one in enumerate(maps):
        total = total + jnp.where(one, 1.0 if scales is None else scales[k : k + 1, :], 0.0)
    return total.astype(jnp.bfloat16)


def dispatch_kernel(experts, capacity, routes_ref, *refs):
    scale_refs, (source_ref, out_ref) = refs[:-2], refs[-2:]
    maps = slot_maps(routes_ref[...], experts, capacity)
    scales = scale_refs[0][...].astype(jnp.float32) if scale_refs else None
    picked = product(weighted_map(maps, scales), source_ref[...])
    out_ref[...] = as_blocks(picked).astype(jnp.bfloat16)


def combine_kernel(experts, capacity, routes_ref, scale_ref, back_ref, cot_ref, mixed_ref, dots_ref):
    maps = slot_maps(routes_ref[...], experts, capacity)
    scales = scale_ref[...].astype(jnp.float32)
    back = as_rows(back_ref[...], cot_ref.shape[1])
    mixed_ref[...] = product(weighted_map(maps, scales), back, ROWS_0).astype(jnp.bfloat16)
    meets = product(back, cot_ref[...], TURNED)
    for k, one in enumerate(maps):
        dots_ref[k : k + 1, :] = jnp.sum(jnp.where(one, meets, 0.0), axis=0, keepdims=True)


def split_halves(total, core):
    half = total.shape[0] // 2
    first, second = total[:half], total[half:]
    return jnp.where(core == 0, first, second), jnp.where(core == 0, second, first)


def pre_kernel(place_ref, x_ref, gate_ref, up_ref, _, mine_ref, theirs_ref, rows_ref):
    @pl.when(pl.program_id(0) == 0)
    def _():
        rows_ref[...] = as_rows(x_ref[...], rows_ref.shape[1])

    for k, w_ref in enumerate((gate_ref, up_ref)):
        mine, theirs = split_halves(product(rows_ref[...], w_ref[0]), place_ref[0])
        mine_ref[k] = mine.astype(jnp.bfloat16)
        theirs_ref[k] = theirs.astype(jnp.bfloat16)


def pre_products(place, x_blocks, w_gate, w_up, behind):
    _, depth, width = w_gate.shape
    rows = x_blocks.size // depth
    half, step = rows // 2, width // 3
    w_spec = pl.BlockSpec((1, depth, step), lambda i, place: (0, 0, i))
    out_spec = pl.BlockSpec((2, half, step), lambda i, place: (0, 0, i))
    return pallas(
        pre_kernel,
        (
            jax.ShapeDtypeStruct((2, half, width), jnp.bfloat16),
            jax.ShapeDtypeStruct((2, half, width), jnp.bfloat16),
            jax.ShapeDtypeStruct((rows, depth), jnp.bfloat16),
        ),
        grid_spec=pltpu.PrefetchScalarGridSpec(
            num_scalar_prefetch=1,
            grid=(3,),
            in_specs=[
                pl.BlockSpec(x_blocks.shape, lambda i, place: (0, 0)),
                w_spec,
                w_spec,
                ANYWHERE,
            ],
            out_specs=(out_spec, out_spec, pl.BlockSpec((rows, depth), lambda i, place: (0, 0))),
        ),
    )(place, x_blocks, in_hbm(w_gate), in_hbm(w_up), behind)


def slope_kernel(place_ref, cot_ref, w_ref, _, mine_ref, theirs_ref):
    total = product(as_rows(cot_ref[...], w_ref.shape[2]), w_ref[0], TURNED)
    mine, theirs = split_halves(total, place_ref[0])
    mine_ref[...] = mine.astype(jnp.bfloat16)
    theirs_ref[...] = theirs.astype(jnp.bfloat16)


def slope_products(place, cot_blocks, w_down, behind):
    half = cot_blocks.size // w_down.shape[2] // 2
    shape = (half, w_down.shape[1])
    return pallas(
        slope_kernel,
        (jax.ShapeDtypeStruct(shape, jnp.bfloat16),) * 2,
        in_specs=[pl.BlockSpec(memory_space=pltpu.SMEM), IN_VMEM, IN_VMEM, ANYWHERE],
        out_specs=(IN_VMEM, IN_VMEM),
    )(place, cot_blocks, w_down, behind)


def chip_sum_kernel(mine_ref, got_ref, out_ref):
    total = mine_ref[...].astype(jnp.float32) + got_ref[...].astype(jnp.float32)
    out_ref[...] = total.astype(jnp.bfloat16)


def chip_sum(mine, got):
    return pallas(
        chip_sum_kernel,
        jax.ShapeDtypeStruct(got.shape, got.dtype),
        in_specs=[IN_VMEM, IN_VMEM],
        out_specs=IN_VMEM,
    )(mine, got)


def gated(pre_ref, pre_got_ref):
    pre_gate = pre_ref[0].astype(jnp.float32) + pre_got_ref[0].astype(jnp.float32)
    pre_up = pre_ref[1].astype(jnp.float32) + pre_got_ref[1].astype(jnp.float32)
    return pre_gate, pre_up, jax.nn.sigmoid(pre_gate)


def hidden_kernel(pre_ref, pre_got_ref, _, out_ref):
    pre_gate, pre_up, sig_gate = gated(pre_ref, pre_got_ref)
    out_ref[...] = (pre_gate * sig_gate * pre_up).astype(jnp.bfloat16)


def out_kernel(place_ref, own_ref, other_ref, w_ref, _, out_ref):
    own, other = own_ref[...], other_ref[...]
    core = place_ref[0]
    hidden = jnp.concatenate(
        [jnp.where(core == 0, own, other), jnp.where(core == 0, other, own)], axis=0
    )
    out_ref[...] = as_blocks(product(hidden, w_ref[0])).astype(jnp.bfloat16)


def out_products(place, own, other, w_down, behind):
    size = 2 * own.shape[0] * w_down.shape[2]
    return pallas(
        out_kernel,
        jax.ShapeDtypeStruct((size // LANES, LANES), jnp.bfloat16),
        in_specs=[pl.BlockSpec(memory_space=pltpu.SMEM), IN_VMEM, IN_VMEM, IN_VMEM, ANYWHERE],
        out_specs=IN_VMEM,
    )(place, own, other, w_down, behind)


def slopes_kernel(groups, place_ref, pre_ref, pre_got_ref, slope_ref, slope_got_ref, out_ref):
    pre_gate, pre_up, sig_gate = gated(pre_ref, pre_got_ref)
    d_hidden = slope_ref[...].astype(jnp.float32) + slope_got_ref[...].astype(jnp.float32)
    d_up = d_hidden * (pre_gate * sig_gate)
    d_gate = d_hidden * pre_up * sig_gate * (1.0 + pre_gate * (1.0 - sig_gate))
    half, width = d_up.shape
    fold, part = half // 2, width // groups
    for j in range(groups):
        cols = slice(j * part, (j + 1) * part)
        chunk = jnp.concatenate(
            [d_gate[:fold, cols], d_up[:fold, cols], d_gate[fold:, cols], d_up[fold:, cols]],
            axis=1,
        )
        out_ref[lax.rem(j - place_ref[1] + groups, groups)] = chunk.astype(jnp.bfloat16)


def slopes(place, pre, pre_got, slope, slope_got, groups):
    half, width = slope.shape
    return pallas(
        functools.partial(slopes_kernel, groups),
        jax.ShapeDtypeStruct((groups, half // 2, 4 * width // groups), jnp.bfloat16),
        in_specs=[pl.BlockSpec(memory_space=pltpu.SMEM)] + [IN_VMEM] * 4,
        out_specs=IN_VMEM,
    )(place, pre, pre_got, slope, slope_got)


def collect_kernel(*refs):
    for part_ref, out_ref in zip(refs[:-2], [refs[-1].at[s] for s in range(len(refs) - 2)]):
        out_ref[...] = part_ref[...]


def collect(parts, behind):
    return pallas(
        collect_kernel,
        jax.ShapeDtypeStruct((len(parts), *parts[0].shape), parts[0].dtype),
        in_specs=[IN_VMEM] * len(parts) + [ANYWHERE],
        out_specs=IN_VMEM,
    )(*parts, behind)


def grads_kernel(with_add, groups, _, *refs):
    x_refs, d_ref, add_refs = refs[:groups], refs[groups], refs[groups + 1 : -2]
    rows = jnp.concatenate([x_ref[0] for x_ref in x_refs], axis=0)
    part = refs[-1].shape[0]
    for fold in range(2):

        @pl.when(pl.program_id(0) == fold)
        def _(fold=fold):
            cols = slice(2 * fold * part, 2 * (fold + 1) * part)
            d = jnp.concatenate([d_ref[s][:, cols] for s in range(groups)], axis=0)
            total = product(d, rows, ROWS_0)
            for k, out_ref in enumerate(refs[-2:]):
                term = total[k * part : (k + 1) * part]
                if fold:
                    term = term + out_ref[...]
                elif with_add:
                    term = term + add_refs[k][...]
                out_ref[...] = term


def weight_grads(place, own, x_parts, d_got, add=()):
    groups, fold, packed = d_got.shape
    width = x_parts[0].shape[1]
    part = packed // 4
    x_spec = pl.BlockSpec((1, fold, width), lambda i, place: (place[0] if own else 1 - place[0], i, 0))
    out_spec = pl.BlockSpec((part, width), lambda i, place: (0, 0))
    return pallas(
        functools.partial(grads_kernel, bool(add), groups),
        (jax.ShapeDtypeStruct((part, width), jnp.float32),) * 2,
        grid_spec=pltpu.PrefetchScalarGridSpec(
            num_scalar_prefetch=1,
            grid=(2,),
            in_specs=[x_spec] * groups
            + [pl.BlockSpec(d_got.shape, lambda i, place: (0, 0, 0))]
            + [out_spec] * len(add),
            out_specs=(out_spec, out_spec),
        ),
    )(place, *[part.reshape(2, 2 * fold, width) for part in x_parts], d_got, *add)


def shards(tokens, cotangent, combine_weights, routes, w_gate, w_up, w_down):
    experts = lax.axis_size("ctx")
    groups = lax.axis_size("dp")
    tok_count, top_count = routes.shape
    quarter = tokens.shape[1]
    capacity = 5 * tok_count * top_count // (4 * experts)
    rows = experts * capacity
    place = jnp.stack([lax.axis_index("tp") % 2, lax.axis_index("dp")]).astype(jnp.int32)
    blocks = jax.ShapeDtypeStruct((rows * quarter // LANES, LANES), jnp.bfloat16)

    def over_ctx(flat):
        return exchange(flat.reshape(experts, -1, LANES), "ctx").reshape(flat.shape)

    routes_t, weights_t = in_hbm(routes.T), in_hbm(combine_weights.T)
    dispatch = pallas(functools.partial(dispatch_kernel, experts, capacity), blocks)
    x_got = over_ctx(dispatch(routes_t, in_hbm(tokens)))
    cot_send = dispatch(routes_t, weights_t, in_hbm(cotangent))
    cot_got = over_ctx(cot_send)

    pre_mine, pre_theirs, x_rows = pre_products(place, x_got, w_gate, w_up, cot_send)
    pre = chip_sum(pre_mine, swap(pre_theirs, 1))
    pre_got = swap(pre, 2)
    slope_mine, slope_theirs = slope_products(place, cot_got, w_down, pre)
    slope = chip_sum(slope_mine, swap(slope_theirs, 1))
    slope_got = swap(slope, 2)
    hidden = pallas(
        hidden_kernel,
        jax.ShapeDtypeStruct(pre.shape[1:], jnp.bfloat16),
        in_specs=[IN_VMEM, IN_VMEM, ANYWHERE],
        out_specs=IN_VMEM,
    )(pre, pre_got, slope)
    out_got = over_ctx(out_products(place, hidden, swap(hidden, 1), w_down, slope_got))
    d_send = slopes(place, pre, pre_got, slope, slope_got, groups)
    d_parts = [d_send[0]] + [shift(d_send[s], s) for s in range(1, groups)]

    mixed, dots = pallas(
        functools.partial(combine_kernel, experts, capacity),
        (
            jax.ShapeDtypeStruct(tokens.shape, jnp.bfloat16),
            jax.ShapeDtypeStruct(routes_t.shape, jnp.float32),
        ),
    )(routes_t, weights_t, out_got, in_hbm(cotangent))
    dots = dots + swap(dots, 1)
    dots = dots + swap(dots, 2)
    combine_grads = dots.T.astype(jnp.bfloat16)

    x_parts = [x_rows] + [None] * (groups - 1)
    for way, places in enumerate((1, -1)):
        going = x_rows
        for step, behind in zip(range(1, groups // 2), (pre, hidden, mixed)):
            going = tie(shift(going, places), behind)
            x_parts[step if way == 0 else groups - step] = going
    half = rows // 2
    ahead, back = x_parts[groups // 2 - 1][:half], x_parts[groups // 2 + 1][half:]
    x_parts[groups // 2] = jnp.concatenate([shift(ahead, 1), shift(back, -1)])

    d_got = collect(d_parts, mixed)
    part_grads = weight_grads(place, True, x_parts, d_got)
    grad_gate, grad_up = weight_grads(place, False, x_parts, swap(d_got, 1), part_grads)
    return (mixed, combine_grads, grad_gate.T[None], grad_up.T[None])


def solution(mesh):
    in_specs = (
        P(("dp", "ctx"), "tp"),
        P(("dp", "ctx"), "tp"),
        P(("dp", "ctx"), None),
        P(("dp", "ctx"), None),
        P("ctx", "tp", None),
        P("ctx", "tp", None),
        P("ctx", None, "tp"),
    )
    out_specs = (
        P(("dp", "ctx"), "tp"),
        P(("dp", "ctx"), None),
        P("ctx", "tp", "dp"),
        P("ctx", "tp", "dp"),
    )
    return jax.shard_map(shards, mesh=mesh, in_specs=in_specs, out_specs=out_specs, check_vma=False)
```

```python
import functools

import jax
import jax.numpy as jnp
from jax import lax
from jax.experimental import pallas as pl
from jax.experimental.pallas import tpu as pltpu
from jax.sharding import PartitionSpec as P

LANES = 128
VMEM_LIMIT = 16 * 1024 * 1024
ROWS_0 = (((0,), (0,)), ((), ()))
PLAIN = (((1,), (0,)), ((), ()))
TURNED = (((1,), (1,)), ((), ()))
ANYWHERE = pl.BlockSpec(memory_space=pl.ANY)
IN_VMEM = pl.BlockSpec(memory_space=pltpu.VMEM)


def product(left, right, dims=PLAIN):
    return lax.dot_general(left, right, dims, preferred_element_type=jnp.float32)


def exchange(blocks, axis):
    return lax.all_to_all(blocks, axis, split_axis=0, concat_axis=0, tiled=True)


def swap(value, bit):
    perm = [(i, i ^ bit) for i in range(lax.axis_size("tp"))]
    return lax.ppermute(value, "tp", perm)


def shift(value, places):
    groups = lax.axis_size("dp")
    return lax.ppermute(value, "dp", [(i, (i + places) % groups) for i in range(groups)])


def in_hbm(value):
    return pltpu.with_memory_space_constraint(value, pltpu.HBM)


def pallas(body, out_shape, **given):
    return pl.pallas_call(
        body,
        out_shape=out_shape,
        compiler_params=pltpu.CompilerParams(vmem_limit_bytes=VMEM_LIMIT),
        cost_estimate=pl.CostEstimate(flops=0, bytes_accessed=0, transcendentals=0),
        **given,
    )


def tie(value, *behind):
    return pallas(
        lambda *refs: None,
        jax.ShapeDtypeStruct(value.shape, value.dtype),
        in_specs=[ANYWHERE] * (1 + len(behind)),
        out_specs=ANYWHERE,
        input_output_aliases={0: 0},
    )(value, *behind)


def as_blocks(flat):
    rows, width = flat.shape
    return flat.reshape(rows, width // LANES, LANES).reshape(-1, LANES)


def as_rows(blocks, width):
    return blocks.reshape(-1, width // LANES, LANES).reshape(-1, width)


def slot_maps(routes, experts, capacity):
    top_count, tok_count = routes.shape
    names = [routes[k : k + 1, :] for k in range(top_count)]
    expert_ids = lax.broadcasted_iota(jnp.int32, (experts, tok_count), 0)
    named = [expert_ids == name for name in names]
    both = sum(one.astype(jnp.float32) for one in named).astype(jnp.bfloat16)
    earlier = lax.broadcasted_iota(jnp.int32, (tok_count, tok_count), 0)
    later = lax.broadcasted_iota(jnp.int32, (tok_count, tok_count), 1)
    counts = product(both, (earlier < later).astype(jnp.float32).astype(jnp.bfloat16))
    slot_rows = lax.broadcasted_iota(jnp.int32, (experts * capacity, tok_count), 0)
    maps = []
    for name, one in zip(names, named):
        slots = jnp.sum(jnp.where(one, counts, 0.0), axis=0, keepdims=True)
        maps.append(slot_rows == name * capacity + slots.astype(jnp.int32))
    return maps


def weighted_map(maps, scales):
    total = 0.0
    for k, one in enumerate(maps):
        total = total + jnp.where(one, 1.0 if scales is None else scales[k : k + 1, :], 0.0)
    return total.astype(jnp.bfloat16)


def dispatch_kernel(experts, capacity, routes_ref, *refs):
    scale_refs, (source_ref, out_ref) = refs[:-2], refs[-2:]
    maps = slot_maps(routes_ref[...], experts, capacity)
    scales = scale_refs[0][...].astype(jnp.float32) if scale_refs else None
    picked = product(weighted_map(maps, scales), source_ref[...])
    out_ref[...] = as_blocks(picked).astype(jnp.bfloat16)


def combine_kernel(experts, capacity, routes_ref, scale_ref, back_ref, cot_ref, mixed_ref, dots_ref):
    maps = slot_maps(routes_ref[...], experts, capacity)
    scales = scale_ref[...].astype(jnp.float32)
    back = as_rows(back_ref[...], cot_ref.shape[1])
    mixed_ref[...] = product(weighted_map(maps, scales), back, ROWS_0).astype(jnp.bfloat16)
    meets = product(back, cot_ref[...], TURNED)
    for k, one in enumerate(maps):
        dots_ref[k : k + 1, :] = jnp.sum(jnp.where(one, meets, 0.0), axis=0, keepdims=True)


def split_halves(total, core):
    half = total.shape[0] // 2
    first, second = total[:half], total[half:]
    return jnp.where(core == 0, first, second), jnp.where(core == 0, second, first)


def pre_kernel(place_ref, x_ref, gate_ref, up_ref, _, mine_ref, theirs_ref, rows_ref):
    @pl.when(pl.program_id(0) == 0)
    def _():
        rows_ref[...] = as_rows(x_ref[...], rows_ref.shape[1])

    for k, w_ref in enumerate((gate_ref, up_ref)):
        mine, theirs = split_halves(product(rows_ref[...], w_ref[0]), place_ref[0])
        mine_ref[k] = mine.astype(jnp.bfloat16)
        theirs_ref[k] = theirs.astype(jnp.bfloat16)


def pre_products(place, x_blocks, w_gate, w_up, behind):
    _, depth, width = w_gate.shape
    rows = x_blocks.size // depth
    half, step = rows // 2, width // 3
    w_spec = pl.BlockSpec((1, depth, step), lambda i, place: (0, 0, i))
    out_spec = pl.BlockSpec((2, half, step), lambda i, place: (0, 0, i))
    return pallas(
        pre_kernel,
        (
            jax.ShapeDtypeStruct((2, half, width), jnp.bfloat16),
            jax.ShapeDtypeStruct((2, half, width), jnp.bfloat16),
            jax.ShapeDtypeStruct((rows, depth), jnp.bfloat16),
        ),
        grid_spec=pltpu.PrefetchScalarGridSpec(
            num_scalar_prefetch=1,
            grid=(3,),
            in_specs=[
                pl.BlockSpec(x_blocks.shape, lambda i, place: (0, 0)),
                w_spec,
                w_spec,
                ANYWHERE,
            ],
            out_specs=(out_spec, out_spec, pl.BlockSpec((rows, depth), lambda i, place: (0, 0))),
        ),
    )(place, x_blocks, in_hbm(w_gate), in_hbm(w_up), behind)


def slope_kernel(place_ref, cot_ref, w_ref, _, mine_ref, theirs_ref):
    total = product(as_rows(cot_ref[...], w_ref.shape[2]), w_ref[0], TURNED)
    mine, theirs = split_halves(total, place_ref[0])
    mine_ref[...] = mine.astype(jnp.bfloat16)
    theirs_ref[...] = theirs.astype(jnp.bfloat16)


def slope_products(place, cot_blocks, w_down, behind):
    half = cot_blocks.size // w_down.shape[2] // 2
    shape = (half, w_down.shape[1])
    return pallas(
        slope_kernel,
        (jax.ShapeDtypeStruct(shape, jnp.bfloat16),) * 2,
        in_specs=[pl.BlockSpec(memory_space=pltpu.SMEM), IN_VMEM, IN_VMEM, ANYWHERE],
        out_specs=(IN_VMEM, IN_VMEM),
    )(place, cot_blocks, in_hbm(w_down), behind)


def chip_sum_kernel(mine_ref, got_ref, out_ref):
    total = mine_ref[...].astype(jnp.float32) + got_ref[...].astype(jnp.float32)
    out_ref[...] = total.astype(jnp.bfloat16)


def chip_sum(mine, got):
    return pallas(
        chip_sum_kernel,
        jax.ShapeDtypeStruct(got.shape, got.dtype),
        in_specs=[IN_VMEM, IN_VMEM],
        out_specs=IN_VMEM,
    )(mine, got)


def gated(pre_ref, pre_got_ref):
    pre_gate = pre_ref[0].astype(jnp.float32) + pre_got_ref[0].astype(jnp.float32)
    pre_up = pre_ref[1].astype(jnp.float32) + pre_got_ref[1].astype(jnp.float32)
    return pre_gate, pre_up, jax.nn.sigmoid(pre_gate)


def hidden_kernel(pre_ref, pre_got_ref, _, out_ref):
    pre_gate, pre_up, sig_gate = gated(pre_ref, pre_got_ref)
    out_ref[...] = (pre_gate * sig_gate * pre_up).astype(jnp.bfloat16)


def out_kernel(place_ref, own_ref, other_ref, w_ref, *refs):
    out_ref = refs[-1]
    own, other = own_ref[...], other_ref[...]
    core = place_ref[0]
    hidden = jnp.concatenate(
        [jnp.where(core == 0, own, other), jnp.where(core == 0, other, own)], axis=0
    )
    out_ref[...] = as_blocks(product(hidden, w_ref[0])).astype(jnp.bfloat16)


def out_products(place, own, other, w_down, *behind):
    size = 2 * own.shape[0] * w_down.shape[2]
    return pallas(
        out_kernel,
        jax.ShapeDtypeStruct((size // LANES, LANES), jnp.bfloat16),
        in_specs=[pl.BlockSpec(memory_space=pltpu.SMEM)] + [IN_VMEM] * 3 + [ANYWHERE] * len(behind),
        out_specs=IN_VMEM,
    )(place, own, other, w_down, *behind)


def slopes_kernel(groups, pre_ref, pre_got_ref, slope_ref, slope_got_ref, out_ref):
    pre_gate, pre_up, sig_gate = gated(pre_ref, pre_got_ref)
    d_hidden = slope_ref[...].astype(jnp.float32) + slope_got_ref[...].astype(jnp.float32)
    d_up = d_hidden * (pre_gate * sig_gate)
    d_gate = d_hidden * pre_up * sig_gate * (1.0 + pre_gate * (1.0 - sig_gate))
    half, width = d_up.shape
    fold, part = half // 2, width // groups
    for j in range(groups):
        cols = slice(j * part, (j + 1) * part)
        chunk = jnp.concatenate(
            [d_gate[:fold, cols], d_up[:fold, cols], d_gate[fold:, cols], d_up[fold:, cols]],
            axis=1,
        )
        out_ref[j] = chunk.astype(jnp.bfloat16)


def slopes(pre, pre_got, slope, slope_got, groups):
    half, width = slope.shape
    return pallas(
        functools.partial(slopes_kernel, groups),
        jax.ShapeDtypeStruct((groups, half // 2, 4 * width // groups), jnp.bfloat16),
        in_specs=[IN_VMEM] * 4,
        out_specs=IN_VMEM,
    )(pre, pre_got, slope, slope_got)


def grads_kernel(with_add, groups, place_ref, *refs):
    x_refs, d_ref, add_refs = refs[:groups], refs[groups], refs[groups + 1 : -2]
    rows = jnp.concatenate([x_ref[0] for x_ref in x_refs], axis=0)
    part = refs[-1].shape[0]
    for fold in range(2):

        @pl.when(pl.program_id(0) == fold)
        def _(fold=fold):
            cols = slice(2 * fold * part, 2 * (fold + 1) * part)
            from_groups = [lax.rem(place_ref[1] - s + groups, groups) for s in range(groups)]
            d = jnp.concatenate([d_ref[g][:, cols] for g in from_groups], axis=0)
            total = product(d, rows, ROWS_0)
            for k, out_ref in enumerate(refs[-2:]):
                term = total[k * part : (k + 1) * part]
                if fold:
                    term = term + out_ref[...]
                elif with_add:
                    term = term + add_refs[k][...]
                out_ref[...] = term


def weight_grads(place, own, x_parts, d_got, add=()):
    groups, fold, packed = d_got.shape
    width = x_parts[0].shape[1]
    part = packed // 4
    x_spec = pl.BlockSpec((1, fold, width), lambda i, place: (place[0] if own else 1 - place[0], i, 0))
    out_spec = pl.BlockSpec((part, width), lambda i, place: (0, 0))
    return pallas(
        functools.partial(grads_kernel, bool(add), groups),
        (jax.ShapeDtypeStruct((part, width), jnp.float32),) * 2,
        grid_spec=pltpu.PrefetchScalarGridSpec(
            num_scalar_prefetch=1,
            grid=(2,),
            in_specs=[x_spec] * groups
            + [pl.BlockSpec(d_got.shape, lambda i, place: (0, 0, 0))]
            + [out_spec] * len(add),
            out_specs=(out_spec, out_spec),
        ),
    )(place, *[in_hbm(part.reshape(2, 2 * fold, width)) for part in x_parts], d_got, *add)


def shards(tokens, cotangent, combine_weights, routes, w_gate, w_up, w_down):
    experts = lax.axis_size("ctx")
    groups = lax.axis_size("dp")
    tok_count, top_count = routes.shape
    quarter = tokens.shape[1]
    capacity = 5 * tok_count * top_count // (4 * experts)
    rows = experts * capacity
    place = jnp.stack([lax.axis_index("tp") % 2, lax.axis_index("dp")]).astype(jnp.int32)
    blocks = jax.ShapeDtypeStruct((rows * quarter // LANES, LANES), jnp.bfloat16)

    def over_ctx(flat):
        return exchange(flat.reshape(experts, -1, LANES), "ctx").reshape(flat.shape)

    routes_t, weights_t = in_hbm(routes.T), in_hbm(combine_weights.T)
    dispatch = pallas(functools.partial(dispatch_kernel, experts, capacity), blocks)
    x_got = over_ctx(dispatch(routes_t, in_hbm(tokens)))
    cot_send = dispatch(routes_t, weights_t, in_hbm(cotangent))
    cot_got = over_ctx(cot_send)

    pre_mine, pre_theirs, x_rows = pre_products(place, x_got, w_gate, w_up, cot_send)
    pre = chip_sum(pre_mine, swap(pre_theirs, 1))
    pre_got = swap(pre, 2)
    slope_mine, slope_theirs = slope_products(place, cot_got, w_down, pre)
    slope = chip_sum(slope_mine, swap(slope_theirs, 1))
    slope_got = swap(slope, 2)
    hidden = pallas(
        hidden_kernel,
        jax.ShapeDtypeStruct(pre.shape[1:], jnp.bfloat16),
        in_specs=[IN_VMEM, IN_VMEM, ANYWHERE],
        out_specs=IN_VMEM,
    )(pre, pre_got, slope)
    first = [shift(x_rows, way) for way in (1, -1)]
    out_send = out_products(place, hidden, swap(hidden, 1), w_down, slope_got, *first)
    out_got = over_ctx(out_send)
    first = [tie(part, out_send) for part in first]
    second = [shift(part, way) for part, way in zip(first, (1, -1))]
    d_send = slopes(pre, pre_got, slope, slope_got, groups)
    second = [tie(part, d_send) for part in second]
    third = [shift(part, way) for part, way in zip(second, (1, -1))]
    d_got = exchange(tie(d_send, out_got, *second), "dp")

    mixed, dots = pallas(
        functools.partial(combine_kernel, experts, capacity),
        (
            jax.ShapeDtypeStruct(tokens.shape, jnp.bfloat16),
            jax.ShapeDtypeStruct(routes_t.shape, jnp.float32),
        ),
    )(routes_t, weights_t, out_got, in_hbm(cotangent))
    dots = dots + swap(dots, 1)
    half = rows // 2
    third = [tie(part, dots) for part in third]
    dots = tie(dots, *third)
    dots = dots + swap(dots, 2)
    combine_grads = dots.T.astype(jnp.bfloat16)

    fourth = jnp.concatenate([shift(third[0][:half], 1), shift(third[1][half:], -1)])
    d_got = tie(d_got, dots, fourth)
    x_parts = [x_rows, first[0], second[0], third[0], fourth, third[1], second[1], first[1]]
    part_grads = weight_grads(place, True, x_parts, d_got)
    grad_gate, grad_up = weight_grads(place, False, x_parts, swap(d_got, 1), part_grads)
    return (mixed, combine_grads, grad_gate.T[None], grad_up.T[None])


def solution(mesh):
    in_specs = (
        P(("dp", "ctx"), "tp"),
        P(("dp", "ctx"), "tp"),
        P(("dp", "ctx"), None),
        P(("dp", "ctx"), None),
        P("ctx", "tp", None),
        P("ctx", "tp", None),
        P("ctx", None, "tp"),
    )
    out_specs = (
        P(("dp", "ctx"), "tp"),
        P(("dp", "ctx"), None),
        P("ctx", "tp", "dp"),
        P("ctx", "tp", "dp"),
    )
    return jax.shard_map(shards, mesh=mesh, in_specs=in_specs, out_specs=out_specs, check_vma=False)
```

```python
import functools

import jax
import jax.numpy as jnp
from jax import lax
from jax.experimental import pallas as pl
from jax.experimental.pallas import tpu as pltpu
from jax.sharding import PartitionSpec as P

LANES = 128
VMEM_LIMIT = 16 * 1024 * 1024
ROWS_0 = (((0,), (0,)), ((), ()))
PLAIN = (((1,), (0,)), ((), ()))
TURNED = (((1,), (1,)), ((), ()))
ANYWHERE = pl.BlockSpec(memory_space=pl.ANY)
IN_VMEM = pl.BlockSpec(memory_space=pltpu.VMEM)


def product(left, right, dims=PLAIN):
    return lax.dot_general(left, right, dims, preferred_element_type=jnp.float32)


def exchange(blocks, axis):
    return lax.all_to_all(blocks, axis, split_axis=0, concat_axis=0, tiled=True)


def swap(value, bit):
    perm = [(i, i ^ bit) for i in range(lax.axis_size("tp"))]
    return lax.ppermute(value, "tp", perm)


def shift(value, places):
    groups = lax.axis_size("dp")
    return lax.ppermute(value, "dp", [(i, (i + places) % groups) for i in range(groups)])


def in_hbm(value):
    return pltpu.with_memory_space_constraint(value, pltpu.HBM)


def pallas(body, out_shape, flops=0, **given):
    return pl.pallas_call(
        body,
        out_shape=out_shape,
        compiler_params=pltpu.CompilerParams(vmem_limit_bytes=VMEM_LIMIT),
        cost_estimate=pl.CostEstimate(flops=flops, bytes_accessed=0, transcendentals=0),
        **given,
    )


def tie(value, *behind):
    return pallas(
        lambda *refs: None,
        jax.ShapeDtypeStruct(value.shape, value.dtype),
        in_specs=[pl.BlockSpec(memory_space=pltpu.HBM)] + [ANYWHERE] * len(behind),
        out_specs=pl.BlockSpec(memory_space=pltpu.HBM),
        input_output_aliases={0: 0},
    )(value, *behind)


def as_blocks(flat):
    rows, width = flat.shape
    return flat.reshape(rows, width // LANES, LANES).reshape(-1, LANES)


def as_rows(blocks, width):
    return blocks.reshape(-1, width // LANES, LANES).reshape(-1, width)


def slot_maps(routes, experts, capacity):
    top_count, tok_count = routes.shape
    names = [routes[k : k + 1, :] for k in range(top_count)]
    expert_ids = lax.broadcasted_iota(jnp.int32, (experts, tok_count), 0)
    named = [expert_ids == name for name in names]
    both = sum(one.astype(jnp.float32) for one in named).astype(jnp.bfloat16)
    earlier = lax.broadcasted_iota(jnp.int32, (tok_count, tok_count), 0)
    later = lax.broadcasted_iota(jnp.int32, (tok_count, tok_count), 1)
    counts = product(both, (earlier < later).astype(jnp.float32).astype(jnp.bfloat16))
    slot_rows = lax.broadcasted_iota(jnp.int32, (experts * capacity, tok_count), 0)
    maps = []
    for name, one in zip(names, named):
        slots = jnp.sum(jnp.where(one, counts, 0.0), axis=0, keepdims=True)
        maps.append(slot_rows == name * capacity + slots.astype(jnp.int32))
    return maps


def weighted_map(maps, scales):
    total = 0.0
    for k, one in enumerate(maps):
        total = total + jnp.where(one, 1.0 if scales is None else scales[k : k + 1, :], 0.0)
    return total.astype(jnp.bfloat16)


def dispatch_kernel(experts, capacity, routes_ref, *refs):
    scale_refs, (source_ref, out_ref) = refs[:-2], refs[-2:]
    maps = slot_maps(routes_ref[...], experts, capacity)
    scales = scale_refs[0][...].astype(jnp.float32) if scale_refs else None
    picked = product(weighted_map(maps, scales), source_ref[...])
    out_ref[...] = as_blocks(picked).astype(jnp.bfloat16)


def combine_kernel(experts, capacity, routes_ref, scale_ref, back_ref, cot_ref, mixed_ref, dots_ref):
    maps = slot_maps(routes_ref[...], experts, capacity)
    scales = scale_ref[...].astype(jnp.float32)
    back = as_rows(back_ref[...], cot_ref.shape[1])
    mixed_ref[...] = product(weighted_map(maps, scales), back, ROWS_0).astype(jnp.bfloat16)
    meets = product(back, cot_ref[...], TURNED)
    for k, one in enumerate(maps):
        dots_ref[k : k + 1, :] = jnp.sum(jnp.where(one, meets, 0.0), axis=0, keepdims=True)


def split_halves(total, core):
    half = total.shape[0] // 2
    first, second = total[:half], total[half:]
    return jnp.where(core == 0, first, second), jnp.where(core == 0, second, first)


def pre_kernel(place_ref, x_ref, gate_ref, up_ref, _, mine_ref, theirs_ref, rows_ref):
    @pl.when(pl.program_id(0) == 0)
    def _():
        rows_ref[...] = as_rows(x_ref[...], rows_ref.shape[1])

    for k, w_ref in enumerate((gate_ref, up_ref)):
        mine, theirs = split_halves(product(rows_ref[...], w_ref[0]), place_ref[0])
        mine_ref[k] = mine.astype(jnp.bfloat16)
        theirs_ref[k] = theirs.astype(jnp.bfloat16)


def pre_products(place, x_blocks, w_gate, w_up, behind):
    _, depth, width = w_gate.shape
    rows = x_blocks.size // depth
    half, step = rows // 2, width // 3
    w_spec = pl.BlockSpec((1, depth, step), lambda i, place: (0, 0, i))
    out_spec = pl.BlockSpec((2, half, step), lambda i, place: (0, 0, i))
    return pallas(
        pre_kernel,
        (
            jax.ShapeDtypeStruct((2, half, width), jnp.bfloat16),
            jax.ShapeDtypeStruct((2, half, width), jnp.bfloat16),
            jax.ShapeDtypeStruct((rows, depth), jnp.bfloat16),
        ),
        grid_spec=pltpu.PrefetchScalarGridSpec(
            num_scalar_prefetch=1,
            grid=(3,),
            in_specs=[
                pl.BlockSpec(x_blocks.shape, lambda i, place: (0, 0)),
                w_spec,
                w_spec,
                ANYWHERE,
            ],
            out_specs=(out_spec, out_spec, pl.BlockSpec((rows, depth), lambda i, place: (0, 0))),
        ),
    )(place, x_blocks, in_hbm(w_gate), in_hbm(w_up), behind)


def slope_kernel(place_ref, cot_ref, w_ref, _, mine_ref, theirs_ref):
    total = product(as_rows(cot_ref[...], w_ref.shape[2]), w_ref[0], TURNED)
    mine, theirs = split_halves(total, place_ref[0])
    mine_ref[...] = mine.astype(jnp.bfloat16)
    theirs_ref[...] = theirs.astype(jnp.bfloat16)


def slope_products(place, cot_blocks, w_down, behind):
    half = cot_blocks.size // w_down.shape[2] // 2
    shape = (half, w_down.shape[1])
    return pallas(
        slope_kernel,
        (jax.ShapeDtypeStruct(shape, jnp.bfloat16),) * 2,
        in_specs=[pl.BlockSpec(memory_space=pltpu.SMEM), IN_VMEM, IN_VMEM, ANYWHERE],
        out_specs=(IN_VMEM, IN_VMEM),
    )(place, cot_blocks, in_hbm(w_down), behind)


def chip_sum_kernel(mine_ref, got_ref, out_ref):
    total = mine_ref[...].astype(jnp.float32) + got_ref[...].astype(jnp.float32)
    out_ref[...] = total.astype(jnp.bfloat16)


def chip_sum(mine, got):
    return pallas(
        chip_sum_kernel,
        jax.ShapeDtypeStruct(got.shape, got.dtype),
        in_specs=[IN_VMEM, IN_VMEM],
        out_specs=IN_VMEM,
    )(mine, got)


def gated(pre_ref, pre_got_ref):
    pre_gate = pre_ref[0].astype(jnp.float32) + pre_got_ref[0].astype(jnp.float32)
    pre_up = pre_ref[1].astype(jnp.float32) + pre_got_ref[1].astype(jnp.float32)
    return pre_gate, pre_up, jax.nn.sigmoid(pre_gate)


def hidden_kernel(pre_ref, pre_got_ref, _, out_ref):
    pre_gate, pre_up, sig_gate = gated(pre_ref, pre_got_ref)
    out_ref[...] = (pre_gate * sig_gate * pre_up).astype(jnp.bfloat16)


def out_kernel(place_ref, own_ref, other_ref, w_ref, *refs):
    out_ref = refs[-1]
    own, other = own_ref[...], other_ref[...]
    core = place_ref[0]
    hidden = jnp.concatenate(
        [jnp.where(core == 0, own, other), jnp.where(core == 0, other, own)], axis=0
    )
    out_ref[...] = as_blocks(product(hidden, w_ref[0])).astype(jnp.bfloat16)


def out_products(place, own, other, w_down, *behind):
    size = 2 * own.shape[0] * w_down.shape[2]
    return pallas(
        out_kernel,
        jax.ShapeDtypeStruct((size // LANES, LANES), jnp.bfloat16),
        in_specs=[pl.BlockSpec(memory_space=pltpu.SMEM)] + [IN_VMEM] * 3 + [ANYWHERE] * len(behind),
        out_specs=IN_VMEM,
    )(place, own, other, w_down, *behind)


def slopes_kernel(groups, pre_ref, pre_got_ref, slope_ref, slope_got_ref, out_ref):
    pre_gate, pre_up, sig_gate = gated(pre_ref, pre_got_ref)
    d_hidden = slope_ref[...].astype(jnp.float32) + slope_got_ref[...].astype(jnp.float32)
    d_up = d_hidden * (pre_gate * sig_gate)
    d_gate = d_hidden * pre_up * sig_gate * (1.0 + pre_gate * (1.0 - sig_gate))
    half, width = d_up.shape
    fold, part = half // 2, width // groups
    for j in range(groups):
        cols = slice(j * part, (j + 1) * part)
        chunk = jnp.concatenate(
            [d_gate[:fold, cols], d_up[:fold, cols], d_gate[fold:, cols], d_up[fold:, cols]],
            axis=1,
        )
        out_ref[j] = chunk.astype(jnp.bfloat16)


def slopes(pre, pre_got, slope, slope_got, groups):
    half, width = slope.shape
    return pallas(
        functools.partial(slopes_kernel, groups),
        jax.ShapeDtypeStruct((groups, half // 2, 4 * width // groups), jnp.bfloat16),
        flops=20 * 10**9,
        in_specs=[IN_VMEM] * 4,
        out_specs=IN_VMEM,
    )(pre, pre_got, slope, slope_got)


def grads_kernel(with_add, groups, place_ref, *refs):
    x_refs, d_ref, add_refs = refs[:groups], refs[groups], refs[groups + 1 : -2]
    rows = jnp.concatenate([x_ref[0] for x_ref in x_refs], axis=0)
    part = refs[-1].shape[0]
    for fold in range(2):

        @pl.when(pl.program_id(0) == fold)
        def _(fold=fold):
            cols = slice(2 * fold * part, 2 * (fold + 1) * part)
            from_groups = [lax.rem(place_ref[1] - s + groups, groups) for s in range(groups)]
            d = jnp.concatenate([d_ref[g][:, cols] for g in from_groups], axis=0)
            total = product(d, rows, ROWS_0)
            for k, out_ref in enumerate(refs[-2:]):
                term = total[k * part : (k + 1) * part]
                if fold:
                    term = term + out_ref[...]
                elif with_add:
                    term = term + add_refs[k][...]
                out_ref[...] = term


def weight_grads(place, own, x_parts, d_got, add=()):
    groups, fold, packed = d_got.shape
    width = x_parts[0].shape[1]
    part = packed // 4
    x_spec = pl.BlockSpec((1, fold, width), lambda i, place: (place[0] if own else 1 - place[0], i, 0))
    out_spec = pl.BlockSpec((part, width), lambda i, place: (0, 0))
    return pallas(
        functools.partial(grads_kernel, bool(add), groups),
        (jax.ShapeDtypeStruct((part, width), jnp.float32),) * 2,
        grid_spec=pltpu.PrefetchScalarGridSpec(
            num_scalar_prefetch=1,
            grid=(2,),
            in_specs=[x_spec] * groups
            + [pl.BlockSpec(d_got.shape, lambda i, place: (0, 0, 0))]
            + [out_spec] * len(add),
            out_specs=(out_spec, out_spec),
        ),
    )(place, *[in_hbm(part.reshape(2, 2 * fold, width)) for part in x_parts], d_got, *add)


def shards(tokens, cotangent, combine_weights, routes, w_gate, w_up, w_down):
    experts = lax.axis_size("ctx")
    groups = lax.axis_size("dp")
    tok_count, top_count = routes.shape
    quarter = tokens.shape[1]
    capacity = 5 * tok_count * top_count // (4 * experts)
    rows = experts * capacity
    place = jnp.stack([lax.axis_index("tp") % 2, lax.axis_index("dp")]).astype(jnp.int32)
    blocks = jax.ShapeDtypeStruct((rows * quarter // LANES, LANES), jnp.bfloat16)

    def over_ctx(flat):
        return exchange(flat.reshape(experts, -1, LANES), "ctx").reshape(flat.shape)

    routes_t, weights_t = in_hbm(routes.T), in_hbm(combine_weights.T)
    dispatch = pallas(functools.partial(dispatch_kernel, experts, capacity), blocks)
    x_got = over_ctx(dispatch(routes_t, in_hbm(tokens)))
    cot_send = dispatch(routes_t, weights_t, in_hbm(cotangent))
    cot_got = over_ctx(cot_send)

    pre_mine, pre_theirs, x_rows = pre_products(place, x_got, w_gate, w_up, cot_send)
    pre = chip_sum(pre_mine, swap(pre_theirs, 1))
    pre_got = swap(pre, 2)
    hidden = pallas(
        hidden_kernel,
        jax.ShapeDtypeStruct(pre.shape[1:], jnp.bfloat16),
        in_specs=[IN_VMEM, IN_VMEM, ANYWHERE],
        out_specs=IN_VMEM,
    )(pre, pre_got, cot_got)
    slope_mine, slope_theirs = slope_products(place, cot_got, w_down, hidden)
    slope = chip_sum(slope_mine, swap(slope_theirs, 1))
    slope_got = swap(slope, 2)

    first = [shift(x_rows, way) for way in (1, -1)]
    first = [tie(part, pre) for part in first]
    second = [shift(part, way) for part, way in zip(first, (1, -1))]
    out_send = out_products(place, hidden, swap(hidden, 1), w_down, slope_theirs)
    out_got = over_ctx(out_send)
    second = [tie(part, hidden) for part in second]
    third = [shift(part, way) for part, way in zip(second, (1, -1))]
    d_send = slopes(pre, pre_got, slope, slope_got, groups)
    d_got = exchange(tie(d_send, out_got), "dp")

    mixed, dots = pallas(
        functools.partial(combine_kernel, experts, capacity),
        (
            jax.ShapeDtypeStruct(tokens.shape, jnp.bfloat16),
            jax.ShapeDtypeStruct(routes_t.shape, jnp.float32),
        ),
    )(routes_t, weights_t, out_got, in_hbm(cotangent))
    dots = dots + swap(dots, 1)
    half = rows // 2
    third = [tie(part, dots) for part in third]
    dots = tie(dots, *third)
    dots = dots + swap(dots, 2)
    combine_grads = dots.T.astype(jnp.bfloat16)

    fourth = jnp.concatenate([shift(third[0][:half], 1), shift(third[1][half:], -1)])
    d_got = tie(d_got, dots, fourth)
    x_parts = [x_rows, first[0], second[0], third[0], fourth, third[1], second[1], first[1]]
    part_grads = weight_grads(place, True, x_parts, d_got)
    grad_gate, grad_up = weight_grads(place, False, x_parts, swap(d_got, 1), part_grads)
    return (mixed, combine_grads, grad_gate.T[None], grad_up.T[None])


def solution(mesh):
    in_specs = (
        P(("dp", "ctx"), "tp"),
        P(("dp", "ctx"), "tp"),
        P(("dp", "ctx"), None),
        P(("dp", "ctx"), None),
        P("ctx", "tp", None),
        P("ctx", "tp", None),
        P("ctx", None, "tp"),
    )
    out_specs = (
        P(("dp", "ctx"), "tp"),
        P(("dp", "ctx"), None),
        P("ctx", "tp", "dp"),
        P("ctx", "tp", "dp"),
    )
    return jax.shard_map(shards, mesh=mesh, in_specs=in_specs, out_specs=out_specs, check_vma=False)
```

```python
import functools

import jax
import jax.numpy as jnp
from jax import lax
from jax.experimental import pallas as pl
from jax.experimental.pallas import tpu as pltpu
from jax.sharding import PartitionSpec as P

LANES = 128
VMEM_LIMIT = 16 * 1024 * 1024
ROWS_0 = (((0,), (0,)), ((), ()))
PLAIN = (((1,), (0,)), ((), ()))
TURNED = (((1,), (1,)), ((), ()))
ANYWHERE = pl.BlockSpec(memory_space=pl.ANY)
IN_VMEM = pl.BlockSpec(memory_space=pltpu.VMEM)


def product(left, right, dims=PLAIN):
    return lax.dot_general(left, right, dims, preferred_element_type=jnp.float32)


def exchange(blocks, axis):
    return lax.all_to_all(blocks, axis, split_axis=0, concat_axis=0, tiled=True)


def swap(value, bit):
    perm = [(i, i ^ bit) for i in range(lax.axis_size("tp"))]
    return lax.ppermute(value, "tp", perm)


def in_hbm(value):
    return pltpu.with_memory_space_constraint(value, pltpu.HBM)


def pallas(body, out_shape, flops=0, **given):
    return pl.pallas_call(
        body,
        out_shape=out_shape,
        compiler_params=pltpu.CompilerParams(vmem_limit_bytes=VMEM_LIMIT),
        cost_estimate=pl.CostEstimate(flops=flops, bytes_accessed=0, transcendentals=0),
        **given,
    )


def tie(value, *behind):
    return pallas(
        lambda *refs: None,
        jax.ShapeDtypeStruct(value.shape, value.dtype),
        in_specs=[ANYWHERE] * (1 + len(behind)),
        out_specs=ANYWHERE,
        input_output_aliases={0: 0},
    )(value, *behind)


def as_blocks(flat):
    rows, width = flat.shape
    return flat.reshape(rows, width // LANES, LANES).reshape(-1, LANES)


def as_rows(blocks, width):
    return blocks.reshape(-1, width // LANES, LANES).reshape(-1, width)


def slot_maps(routes, experts, capacity):
    top_count, tok_count = routes.shape
    names = [routes[k : k + 1, :] for k in range(top_count)]
    expert_ids = lax.broadcasted_iota(jnp.int32, (experts, tok_count), 0)
    named = [expert_ids == name for name in names]
    both = sum(one.astype(jnp.float32) for one in named).astype(jnp.bfloat16)
    earlier = lax.broadcasted_iota(jnp.int32, (tok_count, tok_count), 0)
    later = lax.broadcasted_iota(jnp.int32, (tok_count, tok_count), 1)
    counts = product(both, (earlier < later).astype(jnp.float32).astype(jnp.bfloat16))
    slot_rows = lax.broadcasted_iota(jnp.int32, (experts * capacity, tok_count), 0)
    maps = []
    for name, one in zip(names, named):
        slots = jnp.sum(jnp.where(one, counts, 0.0), axis=0, keepdims=True)
        maps.append(slot_rows == name * capacity + slots.astype(jnp.int32))
    return maps


def weighted_map(maps, scales):
    total = 0.0
    for k, one in enumerate(maps):
        total = total + jnp.where(one, 1.0 if scales is None else scales[k : k + 1, :], 0.0)
    return total.astype(jnp.bfloat16)


def dispatch_kernel(experts, capacity, routes_ref, *refs):
    scale_refs, (source_ref, out_ref) = refs[:-2], refs[-2:]
    maps = slot_maps(routes_ref[...], experts, capacity)
    scales = scale_refs[0][...].astype(jnp.float32) if scale_refs else None
    picked = product(weighted_map(maps, scales), source_ref[...])
    out_ref[...] = as_blocks(picked).astype(jnp.bfloat16)


def combine_kernel(experts, capacity, routes_ref, scale_ref, back_ref, cot_ref, mixed_ref, dots_ref):
    maps = slot_maps(routes_ref[...], experts, capacity)
    scales = scale_ref[...].astype(jnp.float32)
    back = as_rows(back_ref[...], cot_ref.shape[1])
    mixed_ref[...] = product(weighted_map(maps, scales), back, ROWS_0).astype(jnp.bfloat16)
    meets = product(back, cot_ref[...], TURNED)
    for k, one in enumerate(maps):
        dots_ref[k : k + 1, :] = jnp.sum(jnp.where(one, meets, 0.0), axis=0, keepdims=True)


def split_halves(total, core):
    half = total.shape[0] // 2
    first, second = total[:half], total[half:]
    return jnp.where(core == 0, first, second), jnp.where(core == 0, second, first)


def pre_kernel(place_ref, x_ref, gate_ref, up_ref, _, mine_ref, theirs_ref, rows_ref):
    @pl.when(pl.program_id(0) == 0)
    def _():
        rows_ref[...] = as_rows(x_ref[...], rows_ref.shape[1])

    for k, w_ref in enumerate((gate_ref, up_ref)):
        mine, theirs = split_halves(product(rows_ref[...], w_ref[0]), place_ref[0])
        mine_ref[k] = mine.astype(jnp.bfloat16)
        theirs_ref[k] = theirs.astype(jnp.bfloat16)


def pre_products(place, x_blocks, w_gate, w_up, behind):
    _, depth, width = w_gate.shape
    rows = x_blocks.size // depth
    half, step = rows // 2, width // 3
    w_spec = pl.BlockSpec((1, depth, step), lambda i, place: (0, 0, i))
    out_spec = pl.BlockSpec((2, half, step), lambda i, place: (0, 0, i))
    return pallas(
        pre_kernel,
        (
            jax.ShapeDtypeStruct((2, half, width), jnp.bfloat16),
            jax.ShapeDtypeStruct((2, half, width), jnp.bfloat16),
            jax.ShapeDtypeStruct((rows, depth), jnp.bfloat16),
        ),
        grid_spec=pltpu.PrefetchScalarGridSpec(
            num_scalar_prefetch=1,
            grid=(3,),
            in_specs=[
                pl.BlockSpec(x_blocks.shape, lambda i, place: (0, 0)),
                w_spec,
                w_spec,
                ANYWHERE,
            ],
            out_specs=(out_spec, out_spec, pl.BlockSpec((rows, depth), lambda i, place: (0, 0))),
        ),
    )(place, x_blocks, in_hbm(w_gate), in_hbm(w_up), behind)


def slope_kernel(place_ref, cot_ref, w_ref, _, mine_ref, theirs_ref):
    total = product(as_rows(cot_ref[...], w_ref.shape[2]), w_ref[0], TURNED)
    mine, theirs = split_halves(total, place_ref[0])
    mine_ref[...] = mine.astype(jnp.bfloat16)
    theirs_ref[...] = theirs.astype(jnp.bfloat16)


def slope_products(place, cot_blocks, w_down, behind):
    half = cot_blocks.size // w_down.shape[2] // 2
    shape = (half, w_down.shape[1])
    return pallas(
        slope_kernel,
        (jax.ShapeDtypeStruct(shape, jnp.bfloat16),) * 2,
        in_specs=[pl.BlockSpec(memory_space=pltpu.SMEM), IN_VMEM, IN_VMEM, ANYWHERE],
        out_specs=(IN_VMEM, IN_VMEM),
    )(place, cot_blocks, w_down, behind)


def chip_sum_kernel(mine_ref, got_ref, out_ref):
    total = mine_ref[...].astype(jnp.float32) + got_ref[...].astype(jnp.float32)
    out_ref[...] = total.astype(jnp.bfloat16)


def chip_sum(mine, got):
    return pallas(
        chip_sum_kernel,
        jax.ShapeDtypeStruct(got.shape, got.dtype),
        in_specs=[IN_VMEM, IN_VMEM],
        out_specs=IN_VMEM,
    )(mine, got)


def gated(pre_ref, pre_got_ref):
    pre_gate = pre_ref[0].astype(jnp.float32) + pre_got_ref[0].astype(jnp.float32)
    pre_up = pre_ref[1].astype(jnp.float32) + pre_got_ref[1].astype(jnp.float32)
    return pre_gate, pre_up, jax.nn.sigmoid(pre_gate)


def hidden_kernel(pre_ref, pre_got_ref, _, out_ref):
    pre_gate, pre_up, sig_gate = gated(pre_ref, pre_got_ref)
    out_ref[...] = (pre_gate * sig_gate * pre_up).astype(jnp.bfloat16)


def out_kernel(place_ref, own_ref, other_ref, w_ref, _, out_ref):
    own, other = own_ref[...], other_ref[...]
    core = place_ref[0]
    hidden = jnp.concatenate(
        [jnp.where(core == 0, own, other), jnp.where(core == 0, other, own)], axis=0
    )
    out_ref[...] = as_blocks(product(hidden, w_ref[0])).astype(jnp.bfloat16)


def out_products(place, own, other, w_down, behind):
    size = 2 * own.shape[0] * w_down.shape[2]
    return pallas(
        out_kernel,
        jax.ShapeDtypeStruct((size // LANES, LANES), jnp.bfloat16),
        in_specs=[pl.BlockSpec(memory_space=pltpu.SMEM), IN_VMEM, IN_VMEM, IN_VMEM, ANYWHERE],
        out_specs=IN_VMEM,
    )(place, own, other, w_down, behind)


def slopes_kernel(groups, pre_ref, pre_got_ref, slope_ref, slope_got_ref, out_ref):
    pre_gate, pre_up, sig_gate = gated(pre_ref, pre_got_ref)
    d_hidden = slope_ref[...].astype(jnp.float32) + slope_got_ref[...].astype(jnp.float32)
    d_up = d_hidden * (pre_gate * sig_gate)
    d_gate = d_hidden * pre_up * sig_gate * (1.0 + pre_gate * (1.0 - sig_gate))
    half, width = d_up.shape
    fold, part = half // 2, width // groups
    for j in range(groups):
        cols = slice(j * part, (j + 1) * part)
        chunk = jnp.concatenate(
            [d_gate[:fold, cols], d_up[:fold, cols], d_gate[fold:, cols], d_up[fold:, cols]],
            axis=1,
        )
        out_ref[j] = chunk.astype(jnp.bfloat16)


def slopes(pre, pre_got, slope, slope_got, groups):
    half, width = slope.shape
    return pallas(
        functools.partial(slopes_kernel, groups),
        jax.ShapeDtypeStruct((groups, half // 2, 4 * width // groups), jnp.bfloat16),
        flops=20 * 10**9,
        in_specs=[IN_VMEM] * 4,
        out_specs=IN_VMEM,
    )(pre, pre_got, slope, slope_got)


def grads_kernel(with_add, _, x_ref, d_ref, *refs):
    gate_ref, up_ref = refs[-2:]
    count, _, half, width = x_ref.shape
    part = gate_ref.shape[0]
    folds = []
    for g in range(count):
        folds += [d_ref[g][:, : 2 * part], d_ref[g][:, 2 * part :]]
    rows = x_ref[...].reshape(count * half, width)
    total = product(jnp.concatenate(folds, axis=0), rows, ROWS_0)
    first = pl.program_id(0) == 0
    for k, out_ref in enumerate((gate_ref, up_ref)):
        before = jnp.where(first, refs[k][...] if with_add else 0.0, out_ref[...])
        out_ref[...] = before + total[k * part : (k + 1) * part]


def weight_grads(place, own, x_all, d_got, add=()):
    groups, _, half, width = x_all.shape
    _, fold, packed = d_got.shape
    part = packed // 4
    count = groups // 2
    out_spec = pl.BlockSpec((part, width), lambda i, place: (0, 0))
    return pallas(
        functools.partial(grads_kernel, bool(add)),
        (jax.ShapeDtypeStruct((part, width), jnp.float32),) * 2,
        grid_spec=pltpu.PrefetchScalarGridSpec(
            num_scalar_prefetch=1,
            grid=(2,),
            in_specs=[
                pl.BlockSpec(
                    (count, 1, half, width),
                    lambda i, place: (i, place[0] if own else 1 - place[0], 0, 0),
                ),
                pl.BlockSpec((count, fold, packed), lambda i, place: (i, 0, 0)),
            ]
            + [out_spec] * len(add),
            out_specs=(out_spec, out_spec),
        ),
    )(place, in_hbm(x_all), d_got, *add)


def shards(tokens, cotangent, combine_weights, routes, w_gate, w_up, w_down):
    experts = lax.axis_size("ctx")
    groups = lax.axis_size("dp")
    tok_count, top_count = routes.shape
    quarter = tokens.shape[1]
    capacity = 5 * tok_count * top_count // (4 * experts)
    rows = experts * capacity
    place = (lax.axis_index("tp") % 2).astype(jnp.int32)[None]
    blocks = jax.ShapeDtypeStruct((rows * quarter // LANES, LANES), jnp.bfloat16)

    def over_ctx(flat):
        return exchange(flat.reshape(experts, -1, LANES), "ctx").reshape(flat.shape)

    routes_t, weights_t = in_hbm(routes.T), in_hbm(combine_weights.T)
    dispatch = pallas(functools.partial(dispatch_kernel, experts, capacity), blocks)
    x_got = over_ctx(dispatch(routes_t, in_hbm(tokens)))
    cot_send = dispatch(routes_t, weights_t, in_hbm(cotangent))
    cot_got = over_ctx(cot_send)

    pre_mine, pre_theirs, x_rows = pre_products(place, x_got, w_gate, w_up, cot_send)
    x_all = lax.all_gather(x_rows, "dp", axis=0, tiled=True)
    pre = chip_sum(pre_mine, swap(pre_theirs, 1))
    pre_got = swap(pre, 2)
    hidden = pallas(
        hidden_kernel,
        jax.ShapeDtypeStruct(pre.shape[1:], jnp.bfloat16),
        in_specs=[IN_VMEM, IN_VMEM, ANYWHERE],
        out_specs=IN_VMEM,
    )(pre, pre_got, cot_got)
    slope_mine, slope_theirs = slope_products(place, cot_got, w_down, hidden)
    slope_swapped = swap(slope_theirs, 1)
    out_send = out_products(place, hidden, swap(hidden, 1), w_down, slope_theirs)
    out_got = over_ctx(out_send)
    slope = chip_sum(slope_mine, slope_swapped)
    slope_got = swap(slope, 2)
    d_send = slopes(pre, pre_got, slope, slope_got, groups)
    d_got = exchange(tie(d_send, out_got), "dp")

    mixed, dots = pallas(
        functools.partial(combine_kernel, experts, capacity),
        (
            jax.ShapeDtypeStruct(tokens.shape, jnp.bfloat16),
            jax.ShapeDtypeStruct(routes_t.shape, jnp.float32),
        ),
    )(routes_t, weights_t, out_got, in_hbm(cotangent))
    dots = dots + swap(dots, 1)
    dots = dots + swap(dots, 2)
    combine_grads = dots.T.astype(jnp.bfloat16)

    d_got = tie(d_got, dots)
    x_all = x_all.reshape(groups, 2, rows // 2, quarter)
    part_grads = weight_grads(place, True, x_all, d_got)
    grad_gate, grad_up = weight_grads(place, False, x_all, swap(d_got, 1), part_grads)
    return (mixed, combine_grads, grad_gate.T[None], grad_up.T[None])


def solution(mesh):
    in_specs = (
        P(("dp", "ctx"), "tp"),
        P(("dp", "ctx"), "tp"),
        P(("dp", "ctx"), None),
        P(("dp", "ctx"), None),
        P("ctx", "tp", None),
        P("ctx", "tp", None),
        P("ctx", None, "tp"),
    )
    out_specs = (
        P(("dp", "ctx"), "tp"),
        P(("dp", "ctx"), None),
        P("ctx", "tp", "dp"),
        P("ctx", "tp", "dp"),
    )
    return jax.shard_map(shards, mesh=mesh, in_specs=in_specs, out_specs=out_specs, check_vma=False)
```
